32 devices in a mesh: tm: 4 (over z), row: 4 (over y, core), col: 2 (over x).
Axes of the slice: x: 2, y: 2, z: 4, core: 2. Of those that a mesh axis runs over, the one named last changes fastest.
Arguments:
- c_occ: float32 [1536, 1536], P(None, 'tm'), may hold values from -1 to 1
- c_vir: float32 [1536, 1536], P(None, 'tm'), may hold values from -1 to 1
- eps_occ: float32 [1536], P('tm'), may hold values from -1.6 to -0.05, as said below
- eps_vir: float32 [1536], P('tm'), may hold values from 0.05 to 1.6, as said below
- tau: float32 [4], replicated, may hold values from 0.03 to 10
- tweight: float32 [4], replicated, may hold values from 0.02 to 0.15
- omega: float32 [16], replicated, may hold values from 0.05 to 5
- coulomb: float32 [1536, 1536], replicated, may hold values from -2 to 2
Outputs:
- screened: float32 [16, 1536, 1536], P('tm', 'row', 'col')
The draws below stay inside these ranges and needn't reach their ends.
Inputs may be any that keep to these rules, and one draw needn't show every extreme that they name: `eps_occ`: ascending along the orbital index. `eps_vir`: ascending along the orbital index.
All inputs are finite; a program needn't handle non-finite values.
Results may differ from the reference program's by a relative error of at most 0.00005.
Values sent between devices are 32-bit elements; how exact they have to be, the bound alone decides.
No kernel may reach another device: no remote copies, remote signals or barrier semaphores. Data moves between devices by JAX's collectives and lax.ppermute only.
A program may use at most 128 MiB of HBM per device.

```python
import math
import jax
import jax.numpy as jnp
from jax import lax

N = 1536
NOCC = 1536
NVIR = 1536
TIMES = 4
FREQS = 16


def draw_coulomb(key, part):
    key_off, key_diag = jax.random.split(jax.random.fold_in(key, 11))
    off = jax.random.truncated_normal(key_off, -4.0, 4.0, (N, N), jnp.float32)
    off = (off + off.T) * (0.35 / jnp.sqrt(jnp.float32(N)))
    diagonal = jax.random.uniform(key_diag, (N,), jnp.float32, 1.0, 2.0)
    eye = jnp.eye(N, dtype=jnp.float32)
    return off * (1.0 - eye) + eye * diagonal[None, :]


def window_orbitals(key, rows, width, salt):
    groups = 8
    key_sign, key_shape, key_amp, key_noise = jax.random.split(jax.random.fold_in(key, salt), 4)
    signs = (2 * jax.random.randint(key_sign, (rows, groups), 0, 2) - 1).astype(jnp.float32)
    shape_mag = jax.random.uniform(key_shape, (rows, groups), jnp.float32, 0.5, 1.5)
    amplitude = jax.random.uniform(key_amp, (width,), jnp.float32, 0.5, 1.5)
    noise = jax.random.truncated_normal(key_noise, -4.0, 4.0, (rows, width), jnp.float32)
    member = jnp.arange(width) * groups // width
    onehot = (member[None, :] == jnp.arange(groups)[:, None]).astype(jnp.float32)
    coherent = jnp.dot(signs * shape_mag, onehot) * amplitude[None, :]
    return (0.9 * coherent + 0.7 * noise) / jnp.sqrt(jnp.float32(width))


def energy_ladder(key, count, low, high, salt):
    key_gap = jax.random.fold_in(key, salt)
    gaps = jax.random.uniform(key_gap, (count,), jnp.float32, 0.25, 1.75)
    climb = jnp.cumsum(gaps) - gaps[0]
    values = low + (high - low) * climb / climb[-1]
    return jnp.clip(values, low, high)


def draw_c_occ(key, part):
    return window_orbitals(key, N, NOCC, 41)


def draw_c_vir(key, part):
    return window_orbitals(key, N, NVIR, 43)


def draw_eps_occ(key, part):
    return energy_ladder(key, NOCC, -1.6, -0.05, 51)


def draw_eps_vir(key, part):
    return energy_ladder(key, NVIR, 0.05, 1.6, 53)


def setup_inputs(seed: int = 0) -> dict:
    streams_of = jax.random.split(jax.random.key(seed), 9)
    c_occ = draw_c_occ(jax.random.fold_in(streams_of[8], 71), 0)
    c_vir = draw_c_vir(jax.random.fold_in(streams_of[8], 71), 0)
    eps_occ = draw_eps_occ(jax.random.fold_in(streams_of[8], 71), 0)
    eps_vir = draw_eps_vir(jax.random.fold_in(streams_of[8], 71), 0)
    tau = jnp.clip(jnp.exp(jax.random.uniform(streams_of[4], (TIMES,), jnp.float32, math.log(0.03), math.log(10.0))), 0.03, 10.0)
    tweight = jnp.clip(jnp.exp(jax.random.uniform(streams_of[5], (TIMES,), jnp.float32, math.log(0.02), math.log(0.15))), 0.02, 0.15)
    omega = jnp.clip(jnp.exp(jax.random.uniform(streams_of[6], (FREQS,), jnp.float32, math.log(0.05), math.log(5.0))), 0.05, 5.0)
    coulomb = draw_coulomb(jax.random.fold_in(streams_of[8], 71), 0)
    return dict(c_occ=c_occ, c_vir=c_vir, eps_occ=eps_occ, eps_vir=eps_vir, tau=tau, tweight=tweight, omega=omega, coulomb=coulomb)


HIGH = lax.Precision.HIGHEST


def green_pair(c_occ, c_vir, eps_occ, eps_vir, tau_point):
    factor_occ = jnp.exp(eps_occ * tau_point)
    factor_vir = jnp.exp(-eps_vir * tau_point)
    green_occ = jnp.dot(c_occ * factor_occ[None, :], c_occ.T, precision=HIGH, preferred_element_type=jnp.float32)
    green_vir = jnp.dot(c_vir * factor_vir[None, :], c_vir.T, precision=HIGH, preferred_element_type=jnp.float32)
    return -2.0 * green_occ * green_vir


def reference(c_occ, c_vir, eps_occ, eps_vir, tau, tweight, omega, coulomb):
    polar_time = lax.map(lambda point: green_pair(c_occ, c_vir, eps_occ, eps_vir, point), tau)
    gamma = tweight[None, :] * jnp.cos(omega[:, None] * tau[None, :])

    def per_freq(weights):
        polar = jnp.tensordot(weights, polar_time, axes=1, precision=HIGH)
        coupled = jnp.dot(coulomb, polar, precision=HIGH, preferred_element_type=jnp.float32)
        first = coulomb + jnp.dot(coupled, coulomb, precision=HIGH, preferred_element_type=jnp.float32)
        return jnp.dot(coupled, first, precision=HIGH, preferred_element_type=jnp.float32)

    return lax.map(per_freq, gamma)
```

```python
import functools

import jax
import jax.numpy as jnp
from jax import lax
from jax.experimental import pallas as pl
from jax.experimental.pallas import tpu as pltpu
from jax.sharding import PartitionSpec as P

HIGH = lax.Precision.HIGHEST
F32, BF16 = jnp.float32, jnp.bfloat16
VMEM_LIMIT = 60 << 20
TILE = 256


def halves(x):
    high = x.astype(BF16)
    return high, (x - high.astype(F32)).astype(BF16)


def dot(a, b):
    return lax.dot_general(a, b, (((1,), (0,)), ((), ())), preferred_element_type=F32)


def dot_t(a, b):
    return lax.dot_general(a, b, (((1,), (1,)), ((), ())), preferred_element_type=F32)


def dot3(a_high, a_low, b_high, b_low):
    return dot(a_high, b_high) + dot(a_low, b_high) + dot(a_high, b_low)


def split_kernel(v_ref, high_ref, low_ref):
    high_ref[...], low_ref[...] = halves(v_ref[...])


def split(v):
    rows, cols = v.shape
    spec = pl.BlockSpec((rows // 4, cols), lambda i: (i, 0))
    return pl.pallas_call(
        split_kernel,
        grid=(4,),
        in_specs=[spec],
        out_specs=[spec] * 2,
        out_shape=[jax.ShapeDtypeStruct((rows, cols), BF16)] * 2,
        compiler_params=pltpu.CompilerParams(vmem_limit_bytes=VMEM_LIMIT),
        name="split_coulomb",
    )(v)


def tile_tables(blocks):
    lists = ([], [])
    for i in range(blocks):
        mine = min(lists, key=len)
        mine.extend((i, j) for j in range(i, blocks))
    count = max(map(len, lists))
    return [tiles + [tiles[-1]] * (count - len(tiles)) for tiles in lists]


def green_kernel(species, pieces, first, last, tab_i, tab_j, fresh, offset, coef, *refs):
    refs = list(refs)
    sources = [refs.pop(0) for _ in range(pieces)]
    factor = refs.pop(0)
    acc_in = None if first else refs.pop(0)
    occ_in = refs.pop(0) if last else None
    outs = [refs.pop(0) for _ in range(2 if last else 1)]
    c_buf, left, right, sem = refs
    step = pl.program_id(0)
    width = c_buf.shape[1]
    times = factor.shape[0]

    @pl.when(step == 0)
    def _():
        copies = []
        if pieces == 1:
            copies.append(pltpu.make_async_copy(sources[0], c_buf, sem))
        else:
            per = sources[0].shape[0]
            rows = sources[0].shape[2]
            for s, source in enumerate(sources):
                for p in range(per):
                    start = pl.multiple_of(offset[s * per + p], 16)
                    copies.append(
                        pltpu.make_async_copy(
                            source.at[p, species], c_buf.at[pl.ds(start, rows), :], sem
                        )
                    )
        for copy in copies:
            copy.start()
        for copy in copies:
            copy.wait()
        high, low = halves(c_buf[...])
        right[:, :width] = high
        right[:, width : 2 * width] = high
        right[:, 2 * width :] = low

    @pl.when(fresh[step] == 1)
    def _():
        row = pl.multiple_of(tab_i[step] * TILE, TILE)
        c = c_buf[pl.ds(row, TILE), :]
        for t in range(times):
            high, low = halves(c * factor[t : t + 1, :])
            s = slice(t * TILE, (t + 1) * TILE)
            left[s, :width] = high
            left[s, width : 2 * width] = low
            left[s, 2 * width :] = high

    col = pl.multiple_of(tab_j[step] * TILE, TILE)
    green = dot_t(left[...], right[pl.ds(col, TILE), :])
    green = green.reshape(1, times, TILE, TILE)
    if not first:
        green = green + acc_in[...]
    if not last:
        outs[0][...] = green
    else:
        for n, out in enumerate(outs):
            total = jnp.zeros((TILE, TILE), F32)
            for t in range(times):
                total = total + coef[n, t] * (occ_in[0, t] * green[0, t])
            out[0] = total


def green_call(species, sources, factor, tables, offset, coef, grid, acc=None, occ=None):
    times, width = factor.shape
    count = tables[0].shape[0]
    first, last = acc is None, occ is not None
    acc_spec = pl.BlockSpec((1, times, TILE, TILE), lambda n, *_: (n, 0, 0, 0))
    tile_spec = pl.BlockSpec((1, TILE, TILE), lambda n, *_: (n, 0, 0))
    args = list(sources) + [factor]
    specs = [pl.BlockSpec(memory_space=pl.ANY)] * len(sources)
    specs += [pl.BlockSpec((times, width), lambda n, *_: (0, 0))]
    aliases = {}
    if not first:
        if not last:
            aliases = {5 + len(args): 0}
        args.append(acc)
        specs.append(acc_spec)
    if last:
        args.append(occ)
        specs.append(acc_spec)
        out_shape = [jax.ShapeDtypeStruct((count, TILE, TILE), F32)] * 2
        out_specs = [tile_spec] * 2
    else:
        out_shape = jax.ShapeDtypeStruct((count, times, TILE, TILE), F32)
        out_specs = acc_spec
    flops = 2 * 3 * count * times * TILE * TILE * width
    return pl.pallas_call(
        functools.partial(green_kernel, species, len(sources), first, last),
        grid_spec=pltpu.PrefetchScalarGridSpec(
            num_scalar_prefetch=5,
            grid=(count,),
            in_specs=specs,
            out_specs=out_specs,
            scratch_shapes=[
                pltpu.VMEM((grid, width), F32),
                pltpu.VMEM((times * TILE, 3 * width), BF16),
                pltpu.VMEM((grid, 3 * width), BF16),
                pltpu.SemaphoreType.DMA,
            ],
        ),
        out_shape=out_shape,
        input_output_aliases=aliases,
        compiler_params=pltpu.CompilerParams(vmem_limit_bytes=VMEM_LIMIT),
        cost_estimate=pl.CostEstimate(flops=flops, bytes_accessed=24 << 20, transcendentals=0),
        name="green_" + ("occ", "vir")[species],
    )(*tables, offset, coef, *args)


def assemble_kernel(tab_i, tab_j, tile_ref, high_ref, low_ref):
    n = pl.program_id(0)
    i = pl.multiple_of(tab_i[n] * TILE, TILE)
    j = pl.multiple_of(tab_j[n] * TILE, TILE)
    tile = tile_ref[0]
    high_ref[pl.ds(i, TILE), pl.ds(j, TILE)], low_ref[pl.ds(i, TILE), pl.ds(j, TILE)] = halves(tile)

    @pl.when(tab_i[n] != tab_j[n])
    def _():
        high, low = halves(tile.T)
        high_ref[pl.ds(j, TILE), pl.ds(i, TILE)] = high
        low_ref[pl.ds(j, TILE), pl.ds(i, TILE)] = low


def assemble(tiles, tab_i, tab_j, grid):
    whole = pl.BlockSpec((grid, grid), lambda n, *_: (0, 0))
    return pl.pallas_call(
        assemble_kernel,
        grid_spec=pltpu.PrefetchScalarGridSpec(
            num_scalar_prefetch=2,
            grid=(tiles.shape[0],),
            in_specs=[pl.BlockSpec((1, TILE, TILE), lambda n, *_: (n, 0, 0))],
            out_specs=[whole] * 2,
        ),
        out_shape=[jax.ShapeDtypeStruct((grid, grid), BF16)] * 2,
        compiler_params=pltpu.CompilerParams(vmem_limit_bytes=VMEM_LIMIT),
        name="assemble_polar",
    )(tab_i, tab_j, tiles)


def chain_kernel(block, at, v_high, v_low, p_high, p_low, near_ref, far_ref, *scratch):
    vh, vl, ph, plo, rh, rl, xf, xh, xl, sem_p, sem_v, sem_r = scratch
    n = vh.shape[0]
    m = rh.shape[0]
    half = near_ref.shape[1]
    count = n // block
    row = pl.multiple_of(at[0], 16)
    row_copies = [
        pltpu.make_async_copy(v_high.at[pl.ds(row, m), :], rh, sem_r.at[0]),
        pltpu.make_async_copy(v_low.at[pl.ds(row, m), :], rl, sem_r.at[1]),
    ]

    def column_copies(pairs, sems, b):
        cols = pl.ds(b * block, block)
        return [
            pltpu.make_async_copy(src.at[:, cols], dst.at[:, cols], sems.at[k, b])
            for k, (src, dst) in enumerate(pairs)
        ]

    p_copies = [column_copies(((p_high, ph), (p_low, plo)), sem_p, b) for b in range(count)]
    v_copies = [column_copies(((v_high, vh), (v_low, vl)), sem_v, b) for b in range(count)]
    for copy in row_copies:
        copy.start()
    for b in range(count):
        for copy in p_copies[b]:
            copy.start()
    for copy in row_copies:
        copy.wait()
    high, low = rh[...], rl[...]
    for b in range(count):
        for copy in p_copies[b]:
            copy.wait()
        for copy in v_copies[b]:
            copy.start()
        s = slice(b * block, (b + 1) * block)
        r = dot3(high, low, ph[:, s], plo[:, s])
        xf[:, s] = r
        xh[:, s], xl[:, s] = halves(r)
    high, low = xh[...], xl[...]
    for b in range(count):
        for copy in v_copies[b]:
            copy.wait()
        s = slice(b * block, (b + 1) * block)
        rh[:, s], rl[:, s] = halves(dot3(high, low, vh[:, s], vl[:, s]))
    high, low = rh[...], rl[...]
    for b in range(count):
        s = slice(b * block, (b + 1) * block)
        xh[:, s], xl[:, s] = halves(xf[:, s] + dot3(high, low, ph[:, s], plo[:, s]))
    high, low = xh[...], xl[...]
    near = pl.multiple_of(at[1] * half, 128)
    far = pl.multiple_of((1 - at[1]) * half, 128)
    for start, out in ((far, far_ref), (near, near_ref)):
        out[...] = dot3(high, low, vh[:, pl.ds(start, half)], vl[:, pl.ds(start, half)])


def chain(at, v_high, v_low, p_high, p_low, rows, cols):
    n = v_high.shape[0]
    block = n // 3 if n % 384 == 0 else n
    count = n // block
    big = pltpu.VMEM((n, n), BF16)
    strip = pltpu.VMEM((rows, n), BF16)
    return pl.pallas_call(
        functools.partial(chain_kernel, block),
        in_specs=[pl.BlockSpec(memory_space=pltpu.SMEM)] + [pl.BlockSpec(memory_space=pl.ANY)] * 4,
        out_specs=[pl.BlockSpec(memory_space=pltpu.VMEM)] * 2,
        out_shape=[jax.ShapeDtypeStruct((rows, cols), F32)] * 2,
        scratch_shapes=[big] * 4
        + [strip] * 2
        + [pltpu.VMEM((rows, n), F32)]
        + [strip] * 2
        + [pltpu.SemaphoreType.DMA((2, count))] * 2
        + [pltpu.SemaphoreType.DMA((2,))],
        compiler_params=pltpu.CompilerParams(vmem_limit_bytes=VMEM_LIMIT),
        cost_estimate=pl.CostEstimate(flops=24 * rows * n * n, bytes_accessed=20 << 20, transcendentals=0),
        name="chain",
    )(at, v_high, v_low, p_high, p_low)


def swap(x, axis, bit):
    size = lax.axis_size(axis)
    return lax.ppermute(x, axis, [(i, i ^ bit) for i in range(size)])


def ring(x, axis):
    size = lax.axis_size(axis)
    return lax.ppermute(x, axis, [(i, (i + 1) % size) for i in range(size)])


def swap_far(x):
    rows, cols = lax.axis_size("row"), lax.axis_size("col")
    pairs = [(r * cols + c, (r ^ 1) * cols + (c ^ 1)) for r in range(rows) for c in range(cols)]
    return lax.ppermute(x, ("row", "col"), pairs)


def on_plane(c_occ, c_vir, eps_occ, eps_vir, tau, tweight, omega, coulomb):
    grid = coulomb.shape[0]
    planes = lax.axis_size("tm")
    rows_n, cols_n = lax.axis_size("row"), lax.axis_size("col")
    z, r, x = lax.axis_index("tm"), lax.axis_index("row"), lax.axis_index("col")
    y, core = r // 2, r % 2
    own = grid // (rows_n * cols_n)
    tile_rows, tile_cols = grid // rows_n, grid // cols_n

    def place(dy, dc, dx):
        return ((((y ^ dy) * 2 + (core ^ dc)) * cols_n) + (x ^ dx)) * own

    shifts = [(0, 0), (0, 1), (1, 0), (1, 1)]
    offset = jnp.stack([place(dy, dc, dx) for dc in range(2) for dy, dx in shifts]).astype(jnp.int32)
    start = place(0, 0, 0)
    piece = jnp.stack(
        [
            lax.dynamic_slice_in_dim(c_occ, start, own, 0),
            lax.dynamic_slice_in_dim(c_vir, start, own, 0),
        ]
    )
    eps = lax.all_gather(jnp.stack([eps_occ, -eps_vir]), "tm", axis=0)
    factors = jnp.exp(eps[:, :, None, :] * tau[None, None, :, None])
    factors_here = jnp.exp(jnp.stack([eps_occ, -eps_vir])[:, None, :] * tau[None, :, None])

    gamma = tweight[None, :] * jnp.cos(omega[:, None] * tau[None, :])
    per_plane = omega.shape[0] // planes
    mine = z * per_plane + x * 2 + core
    other = z * per_plane + x * 2 + 1 - core
    coef = -2.0 * jnp.stack([gamma[mine], gamma[other]])

    lists = tile_tables(grid // TILE)
    tab = jnp.array(lists, jnp.int32)
    fresh = jnp.array(
        [[int(n == 0 or t[n][0] != t[n - 1][0]) for n in range(len(t))] for t in lists], jnp.int32
    )
    tables = (tab[core, :, 0], tab[core, :, 1], fresh[core])
    tab_both = jnp.concatenate([tab[core], tab[1 - core]])

    v_high, v_low = split(coulomb)
    acc = [
        green_call(s, [c], factors_here[s], tables, offset, coef, grid)
        for s, c in enumerate((c_occ, c_vir))
    ]
    for t in range(1, planes):
        piece = ring(piece, "tm")
        by_x = swap(piece, "col", 1)
        by_y = swap(piece, "row", 2)
        far_occ = swap(by_x[0], "row", 2)
        far_vir = swap(by_y[1], "col", 1)
        chip = jnp.stack([piece, by_x, by_y, jnp.stack([far_occ, far_vir])])
        chips = [chip, swap(chip, "row", 1)]
        factor = factors[(z - t) % planes]
        if t < planes - 1:
            acc = [
                green_call(s, chips, factor[s], tables, offset, coef, grid, acc[s])
                for s in range(2)
            ]
        else:
            acc[0] = green_call(0, chips, factor[0], tables, offset, coef, grid, acc[0])
            mine_tiles, other_tiles = green_call(
                1, chips, factor[1], tables, offset, coef, grid, acc[1], acc[0]
            )
    tiles = jnp.concatenate([mine_tiles, swap(other_tiles, "row", 1)])
    p_high, p_low = assemble(tiles, tab_both[:, 0], tab_both[:, 1], grid)

    out = jnp.zeros((per_plane, tile_rows, tile_cols), F32)

    def put(out, value, dx, dc):
        return lax.dynamic_update_slice(out, value[None], ((x ^ dx) * 2 + (core ^ dc), 0, 0))

    for dc in range(2):
        at = jnp.stack([(y * 2 + (core ^ dc)) * tile_rows, x]).astype(jnp.int32)
        near, far = chain(at, v_high, v_low, p_high, p_low, tile_rows, tile_cols)
        if dc == 0:
            out = put(out, near, 0, 0)
            out = put(out, swap(far, "col", 1), 1, 0)
        else:
            out = put(out, swap(near, "row", 1), 0, 1)
            out = put(out, swap_far(far), 1, 1)
    return out


def green_block(rows_c, cols_c, energies, taus, sign):
    factor = jnp.exp(sign * taus[:, None] * energies[None, :])
    width = rows_c.shape[1]
    scaled = rows_c[:, None, :] * factor[None, :, :]
    lead = (rows_c.shape[0], taus.shape[0])
    flat = scaled.reshape(lead[0] * lead[1], width)
    product = lax.dot_general(
        flat, cols_c, (((1,), (1,)), ((), ())), precision=HIGH, preferred_element_type=F32
    )
    return product.reshape(lead[0], lead[1], cols_c.shape[0])


def on_device(c_occ, c_vir, eps_occ, eps_vir, tau, tweight, omega, coulomb):
    grid = coulomb.shape[0]
    tile_rows = grid // lax.axis_size("row")
    tile_cols = grid // lax.axis_size("col")
    row_start = lax.axis_index("row") * tile_rows
    col_start = lax.axis_index("col") * tile_cols
    occ_rows = lax.dynamic_slice_in_dim(c_occ, row_start, tile_rows, 0)
    occ_cols = lax.dynamic_slice_in_dim(c_occ, col_start, tile_cols, 0)
    vir_rows = lax.dynamic_slice_in_dim(c_vir, row_start, tile_rows, 0)
    vir_cols = lax.dynamic_slice_in_dim(c_vir, col_start, tile_cols, 0)
    gamma = tweight[None, :] * jnp.cos(omega[:, None] * tau[None, :])
    green_occ = green_block(occ_rows, occ_cols, eps_occ, tau, 1.0)
    green_vir = green_block(vir_rows, vir_cols, eps_vir, tau, -1.0)
    greens = lax.psum_scatter(
        jnp.stack([green_occ, green_vir], axis=1), "tm", scatter_dimension=0, tiled=True
    )
    polar_time = -2.0 * greens[:, 0] * greens[:, 1]
    polar_all = jnp.einsum("kj,ijc->kic", gamma, polar_time, precision=HIGH)
    polar = lax.all_to_all(polar_all, "tm", split_axis=0, concat_axis=1, tiled=True)
    coulomb_rows = lax.dynamic_slice_in_dim(coulomb, row_start, tile_rows, 0)
    coulomb_cols = lax.dynamic_slice_in_dim(coulomb, col_start, tile_cols, 1)
    coulomb_tile = lax.dynamic_slice_in_dim(coulomb_rows, col_start, tile_cols, 1)
    coupled = jnp.einsum(
        "ik,fkj->fij", coulomb_rows, lax.all_gather(polar, "row", axis=1, tiled=True), precision=HIGH
    )
    coupled_rows = lax.all_gather(coupled, "col", axis=2, tiled=True)
    first = coulomb_tile[None] + jnp.einsum(
        "fik,kj->fij", coupled_rows, coulomb_cols, precision=HIGH
    )
    return jnp.einsum(
        "fik,fkj->fij", coupled_rows, lax.all_gather(first, "row", axis=1, tiled=True), precision=HIGH
    )


def solution(mesh):
    in_specs = (P(None, "tm"), P(None, "tm"), P("tm"), P("tm"), P(), P(), P(), P())
    out_specs = P("tm", "row", "col")
    square = mesh.shape["row"] == 4 and mesh.shape["col"] == 2

    def body(*args):
        omega, coulomb = args[6], args[7]
        fits = omega.shape[0] == 2 * mesh.shape["tm"] * mesh.shape["col"]
        fits = fits and coulomb.shape[0] % (2 * TILE) == 0 and args[0].shape[1] % 128 == 0
        return (on_plane if square and fits else on_device)(*args)

    return jax.shard_map(
        body, mesh=mesh, in_specs=in_specs, out_specs=out_specs, check_vma=False
    )
```

```python
import functools

import jax
import jax.numpy as jnp
import numpy as np
from jax import lax
from jax.experimental import pallas as pl
from jax.experimental.pallas import tpu as pltpu
from jax.sharding import PartitionSpec as P

HIGH = lax.Precision.HIGHEST
F32, BF16 = jnp.float32, jnp.bfloat16
VMEM_LIMIT = 60 << 20
TILE = 256


def halves(x):
    high = x.astype(BF16)
    return high, (x - high.astype(F32)).astype(BF16)


def dot(a, b):
    return lax.dot_general(a, b, (((1,), (0,)), ((), ())), preferred_element_type=F32)


def dot_t(a, b):
    return lax.dot_general(a, b, (((1,), (1,)), ((), ())), preferred_element_type=F32)


def dot3(a_high, a_low, b_high, b_low):
    return dot(a_high, b_high) + dot(a_low, b_high) + dot(a_high, b_low)


def split_kernel(v_ref, high_ref, low_ref):
    high_ref[...], low_ref[...] = halves(v_ref[...])


def split(v):
    rows, cols = v.shape
    spec = pl.BlockSpec((rows // 4, cols), lambda i: (i, 0))
    return pl.pallas_call(
        split_kernel,
        grid=(4,),
        in_specs=[spec],
        out_specs=[spec] * 2,
        out_shape=[jax.ShapeDtypeStruct((rows, cols), BF16)] * 2,
        compiler_params=pltpu.CompilerParams(vmem_limit_bytes=VMEM_LIMIT),
        name="split_coulomb",
    )(v)


def green_kernel(merged, first, last, meta, coef, *refs):
    refs = list(refs)
    sources = [refs.pop(0) for _ in range(merged or 1)]
    factor = refs.pop(0)
    acc_in = None if first else refs.pop(0)
    occ_in = refs.pop(0) if last else None
    outs = [refs.pop(0) for _ in range(coef.shape[0] if last else 1)]
    c_buf, left, right, sem = refs
    step = pl.program_id(0)
    width = c_buf.shape[1]
    times = factor.shape[0]
    strip = left.shape[0] // times
    size = c_buf.shape[0] // 3

    @pl.when(step == 0)
    def _():
        copies = []
        for k, source in enumerate(sources):
            for s in range(3):
                if merged:
                    rows, part = source.shape[1:]
                    start = pl.multiple_of(meta[k % 2], 16) + s * size
                    here = c_buf.at[pl.ds(start, rows), pl.ds(k // 2 * part, part)]
                    copies.append(pltpu.make_async_copy(source.at[s], here, sem))
                else:
                    start = pl.multiple_of(meta[2 + s], 16)
                    here = c_buf.at[pl.ds(s * size, size), :]
                    copies.append(pltpu.make_async_copy(source.at[pl.ds(start, size), :], here, sem))
        for copy in copies:
            copy.start()
        for copy in copies:
            copy.wait()
        high, low = halves(c_buf[...])
        right[:, :width] = high
        right[:, width : 2 * width] = high
        right[:, 2 * width :] = low

    c = c_buf[pl.ds(pl.multiple_of(meta[5 + step], 16), strip), :]
    for t in range(times):
        high, low = halves(c * factor[t : t + 1, :])
        s = slice(t * strip, (t + 1) * strip)
        left[s, :width] = high
        left[s, width : 2 * width] = low
        left[s, 2 * width :] = high

    row = pl.multiple_of(meta[10 + step], 128)
    green = dot_t(left[...], right[pl.ds(row, size), :])
    green = green.reshape(1, times, strip, size)
    if not first:
        green = green + acc_in[...]
    if not last:
        outs[0][...] = green
    else:
        pairs = [occ_in[0, t] * green[0, t] for t in range(times)]
        for n, out in enumerate(outs):
            total = coef[n, 0] * pairs[0]
            for t in range(1, times):
                total = total + coef[n, t] * pairs[t]
            out[0] = total


def green_call(name, sources, factor, meta, coef, size, acc=None, occ=None):
    times, width = factor.shape
    strip = size // 4
    first, last = acc is None, occ is not None
    merged = len(sources) if len(sources) > 1 else 0
    acc_spec = pl.BlockSpec((1, times, strip, size), lambda n, *_: (n, 0, 0, 0))
    part_spec = pl.BlockSpec((1, strip, size), lambda n, *_: (n, 0, 0))
    args = list(sources) + [factor]
    specs = [pl.BlockSpec(memory_space=pl.ANY)] * len(sources)
    specs += [pl.BlockSpec((times, width), lambda n, *_: (0, 0))]
    aliases = {}
    if not first:
        if not last:
            aliases = {2 + len(args): 0}
        args.append(acc)
        specs.append(acc_spec)
    if last:
        args.append(occ)
        specs.append(acc_spec)
        out_shape = [jax.ShapeDtypeStruct((5, strip, size), F32)] * coef.shape[0]
        out_specs = [part_spec] * coef.shape[0]
    else:
        out_shape = jax.ShapeDtypeStruct((5, times, strip, size), F32)
        out_specs = acc_spec
    return pl.pallas_call(
        functools.partial(green_kernel, merged, first, last),
        grid_spec=pltpu.PrefetchScalarGridSpec(
            num_scalar_prefetch=2,
            grid=(5,),
            in_specs=specs,
            out_specs=out_specs,
            scratch_shapes=[
                pltpu.VMEM((3 * size, width), F32),
                pltpu.VMEM((times * strip, 3 * width), BF16),
                pltpu.VMEM((3 * size, 3 * width), BF16),
                pltpu.SemaphoreType.DMA,
            ],
        ),
        out_shape=out_shape,
        input_output_aliases=aliases,
        compiler_params=pltpu.CompilerParams(vmem_limit_bytes=VMEM_LIMIT),
        cost_estimate=pl.CostEstimate(
            flops=6 * 5 * times * strip * size * width, bytes_accessed=12 << 20, transcendentals=0
        ),
        name=name,
    )(meta, coef, *args)


def chain_kernel(block, *refs):
    at, spots = refs[:2]
    parts, (v_high, v_low, near_ref, far_ref) = refs[2:10], refs[10:14]
    vh, vl, pf, ph, plo, rh, rl, xf, xh, xl, sem_p, sem_v, sem_r = refs[14:]
    n = vh.shape[0]
    m = rh.shape[0]
    half = far_ref.shape[1]
    count, strip, size = parts[0].shape
    row = pl.multiple_of(at[0], 16)
    row_copies = [
        pltpu.make_async_copy(v_high.at[pl.ds(row, m), :], rh, sem_r.at[0]),
        pltpu.make_async_copy(v_low.at[pl.ds(row, m), :], rl, sem_r.at[1]),
    ]
    p_copies = []
    for k, part in enumerate(parts):
        for t in range(count):
            i = pl.multiple_of(spots[2 * (k * count + t)], 16)
            j = pl.multiple_of(spots[2 * (k * count + t) + 1], 128)
            there = pf.at[pl.ds(i, strip), pl.ds(j, size)]
            p_copies.append(pltpu.make_async_copy(part.at[t], there, sem_p))
    v_copies = []
    for b in range(n // block):
        cols = pl.ds(b * block, block)
        v_copies.append(
            [
                pltpu.make_async_copy(v_high.at[:, cols], vh.at[:, cols], sem_v.at[0, b]),
                pltpu.make_async_copy(v_low.at[:, cols], vl.at[:, cols], sem_v.at[1, b]),
            ]
        )
    for copy in p_copies + row_copies:
        copy.start()
    for copy in p_copies + row_copies:
        copy.wait()
    for pair in v_copies:
        for copy in pair:
            copy.start()
    for b in range(n // block):
        s = slice(b * block, (b + 1) * block)
        for g in range(size, n, size):
            if s.start < g < s.stop:
                pf[g : s.stop, s.start : g] = pf[s.start : g, g : s.stop].T
        ph[: s.stop, s], plo[: s.stop, s] = halves(pf[: s.stop, s])

    def times_p(high, low, b):
        s = slice(b * block, (b + 1) * block)
        r = dot3(high[:, : s.stop], low[:, : s.stop], ph[: s.stop, s], plo[: s.stop, s])
        if s.stop < n:
            h, lo = high[:, s.stop :], low[:, s.stop :]
            ph_t, pl_t = ph[s, s.stop :], plo[s, s.stop :]
            r = r + dot_t(h, ph_t) + dot_t(lo, ph_t) + dot_t(h, pl_t)
        return r

    high, low = rh[...], rl[...]
    for b in range(n // block):
        s = slice(b * block, (b + 1) * block)
        r = times_p(high, low, b)
        xf[:, s] = r
        xh[:, s], xl[:, s] = halves(r)
    high, low = xh[...], xl[...]
    for b in range(n // block):
        for copy in v_copies[b]:
            copy.wait()
        s = slice(b * block, (b + 1) * block)
        rh[:, s], rl[:, s] = halves(dot3(high, low, vh[:, s], vl[:, s]))
    high, low = rh[...], rl[...]
    for b in range(n // block):
        s = slice(b * block, (b + 1) * block)
        xh[:, s], xl[:, s] = halves(xf[:, s] + times_p(high, low, b))
    high, low = xh[...], xl[...]
    near = pl.multiple_of(at[1] * half, 128)
    far = pl.multiple_of((1 - at[1]) * half, 128)
    for start, out in ((far, far_ref), (near, near_ref)):
        out[...] = dot3(high, low, vh[:, pl.ds(start, half)], vl[:, pl.ds(start, half)])


def chain(at, spots, parts, v_high, v_low, rows, cols):
    n = v_high.shape[0]
    block = 2 * TILE
    big = pltpu.VMEM((n, n), BF16)
    strip = pltpu.VMEM((rows, n), BF16)
    smem, hbm = pl.BlockSpec(memory_space=pltpu.SMEM), pl.BlockSpec(memory_space=pl.ANY)
    scratch = [big, big, pltpu.VMEM((n, n), F32), big, big, strip, strip]
    scratch += [pltpu.VMEM((rows, n), F32), strip, strip]
    scratch += [pltpu.SemaphoreType.DMA, pltpu.SemaphoreType.DMA((2, n // block))]
    scratch += [pltpu.SemaphoreType.DMA((2,))]
    return pl.pallas_call(
        functools.partial(chain_kernel, block),
        in_specs=[smem] * 2 + [hbm] * (len(parts) + 2),
        out_specs=[pl.BlockSpec(memory_space=pltpu.VMEM)] * 2,
        out_shape=[jax.ShapeDtypeStruct((rows, cols), F32)] * 2,
        scratch_shapes=scratch,
        compiler_params=pltpu.CompilerParams(vmem_limit_bytes=VMEM_LIMIT),
        cost_estimate=pl.CostEstimate(
            flops=24 * rows * n * n, bytes_accessed=20 << 20, transcendentals=0
        ),
        name="chain",
    )(at, spots, *parts, v_high, v_low)


def move(v, where):
    cols = lax.axis_size("col")
    pairs = []
    for r in range(lax.axis_size("row")):
        for c in range(cols):
            x, y, core = where(c, r // 2, r % 2)
            pairs.append((r * cols + c, (2 * y + core) * cols + x))
    return lax.ppermute(v, ("row", "col"), pairs)


def over(v, dx, dy, dc):
    return move(v, lambda x, y, c: (x ^ dx, y ^ dy, c ^ dc))


def ring(v, steps=1):
    size = lax.axis_size("tm")
    return lax.ppermute(v, "tm", [(i, (i + steps) % size) for i in range(size)])


def after(v, *others):
    return lax.optimization_barrier((v,) + others)[0]


def tables_of(size):
    strip = size // 4
    devices = [(x, y, c) for y in range(2) for c in range(2) for x in range(2)]

    def strips(x, y, c):
        return [2 * c, 2 * c + 1, 2 * x + c, 2 * y + c, 2 * x + c]

    def spots(x, y, c):
        cross = y ^ (1 - x)
        left = [2 * x + y, 2 * x + y, y, 2 * x, cross]
        right = [2 * x + y, 2 * x + y, 2 + y, 2 * x + 1, 3 - cross]
        return [(a * size + t * strip, b * size) for a, b, t in zip(left, right, strips(x, y, c))]

    meta, places = [], []
    for x, y, c in devices:
        sets = [2 * x + y, 2 * (1 - x) + y, 2 * x + 1 - y]
        left, right = [0, 0, x, 2 * y, 2 - x], [0, 0, 1 - x, 2 - 2 * y, 1 + x]
        meta.append(
            [c * 2 * strip, (1 - c) * 2 * strip]
            + [s * size for s in sets]
            + [s * size + t * strip for s, t in zip(left, strips(x, y, c))]
            + [s * size for s in right]
        )
        places.append(
            [spots(x ^ dx, y ^ dy, c ^ dc) for dc in range(2) for dx in range(2) for dy in range(2)]
        )
    flat = np.array(places, np.int32).reshape(len(devices), -1)
    return np.array(meta, np.int32), flat


def on_plane(c_occ, c_vir, eps_occ, eps_vir, tau, tweight, omega, coulomb):
    grid = coulomb.shape[0]
    planes = lax.axis_size("tm")
    rows_n, cols_n = lax.axis_size("row"), lax.axis_size("col")
    z, r, x = lax.axis_index("tm"), lax.axis_index("row"), lax.axis_index("col")
    y, core = r // 2, r % 2
    tile_rows, tile_cols = grid // rows_n, grid // cols_n
    size = grid // 4
    strip = size // 4
    ways = [(dx, dy) for dx in range(2) for dy in range(2)]
    here = (2 * y + core) * cols_n + x
    meta, spots = (jnp.array(t)[here] for t in tables_of(size))

    energies = jnp.stack([eps_occ, -eps_vir])
    arriving = jnp.concatenate([ring(energies, t) for t in range(1, planes)], axis=1)

    def factor(e):
        return jnp.exp(e[None, :] * tau[:, None])

    gamma = tweight[None, :] * jnp.cos(omega[:, None] * tau[None, :])
    per_plane = omega.shape[0] // planes
    coef = -2.0 * jnp.stack(
        [gamma[z * per_plane + 2 * (x ^ dx) + (y ^ dy)] for dx, dy in ways]
    )

    start = (2 * x + y) * size + core * 2 * strip
    common = (meta, coef, size)
    own = [None, None]
    sources = [[], []]
    piece = None
    v_high = v_low = None
    for s, c in enumerate((c_occ, c_vir)):
        before = piece
        piece = lax.dynamic_slice_in_dim(c, start, 2 * strip, 0)
        if before is not None:
            piece = after(piece, before, own[1])
        for t in range(1, planes):
            arrived = piece = ring(piece)
            if s == 0 and t == 1:
                v_high, v_low = split(coulomb)
                piece = after(piece, v_high)
            elif s == 0 and t < 4:
                args = (("green_occ_own", c_occ), ("green_vir_own", c_vir))[t - 2]
                own[t - 2] = green_call(
                    args[0], [after(args[1], arrived)], factor(energies[t - 2]), *common
                )
                piece = after(piece, own[t - 2])
            sets = jnp.stack([arrived, over(arrived, 1, 0, 0), over(arrived, 0, 1, 0)])
            sources[s] += [sets, over(sets, 0, 0, 1)]
    occ = green_call("green_occ", sources[0], factor(arriving[0]), *common, own[0])
    parts = green_call("green_vir", sources[1], factor(arriving[1]), *common, own[1], occ)

    parts = [over(p, dx, dy, 0) if dx + dy else p for p, (dx, dy) in zip(parts, ways)]
    parts += [over(p, 0, 0, 1) for p in parts]

    arrivals = []
    for e in range(2):
        at = jnp.stack([(2 * core + (y ^ e)) * tile_rows, x]).astype(jnp.int32)
        near, far = chain(at, spots, parts, v_high, v_low, tile_rows, tile_cols)
        for dx, value in ((1, far), (0, near)):
            value = move(value, lambda x, y, c, dx=dx, e=e: (x ^ dx, c, y ^ e))
            arrivals.append((2 * (x ^ dx) + (core ^ e), value))
    out = jnp.zeros((per_plane, tile_rows, tile_cols), F32)
    for k, value in arrivals:
        out = lax.dynamic_update_slice(out, value[None], (k, 0, 0))
    return out


def green_block(rows_c, cols_c, energies, taus, sign):
    factor = jnp.exp(sign * taus[:, None] * energies[None, :])
    width = rows_c.shape[1]
    scaled = rows_c[:, None, :] * factor[None, :, :]
    lead = (rows_c.shape[0], taus.shape[0])
    flat = scaled.reshape(lead[0] * lead[1], width)
    product = lax.dot_general(
        flat, cols_c, (((1,), (1,)), ((), ())), precision=HIGH, preferred_element_type=F32
    )
    return product.reshape(lead[0], lead[1], cols_c.shape[0])


def on_device(c_occ, c_vir, eps_occ, eps_vir, tau, tweight, omega, coulomb):
    grid = coulomb.shape[0]
    tile_rows = grid // lax.axis_size("row")
    tile_cols = grid // lax.axis_size("col")
    row_start = lax.axis_index("row") * tile_rows
    col_start = lax.axis_index("col") * tile_cols
    occ_rows = lax.dynamic_slice_in_dim(c_occ, row_start, tile_rows, 0)
    occ_cols = lax.dynamic_slice_in_dim(c_occ, col_start, tile_cols, 0)
    vir_rows = lax.dynamic_slice_in_dim(c_vir, row_start, tile_rows, 0)
    vir_cols = lax.dynamic_slice_in_dim(c_vir, col_start, tile_cols, 0)
    gamma = tweight[None, :] * jnp.cos(omega[:, None] * tau[None, :])
    green_occ = green_block(occ_rows, occ_cols, eps_occ, tau, 1.0)
    green_vir = green_block(vir_rows, vir_cols, eps_vir, tau, -1.0)
    greens = lax.psum_scatter(
        jnp.stack([green_occ, green_vir], axis=1), "tm", scatter_dimension=0, tiled=True
    )
    polar_time = -2.0 * greens[:, 0] * greens[:, 1]
    polar_all = jnp.einsum("kj,ijc->kic", gamma, polar_time, precision=HIGH)
    polar = lax.all_to_all(polar_all, "tm", split_axis=0, concat_axis=1, tiled=True)
    coulomb_rows = lax.dynamic_slice_in_dim(coulomb, row_start, tile_rows, 0)
    coulomb_cols = lax.dynamic_slice_in_dim(coulomb, col_start, tile_cols, 1)
    coulomb_tile = lax.dynamic_slice_in_dim(coulomb_rows, col_start, tile_cols, 1)
    coupled = jnp.einsum(
        "ik,fkj->fij", coulomb_rows, lax.all_gather(polar, "row", axis=1, tiled=True), precision=HIGH
    )
    coupled_rows = lax.all_gather(coupled, "col", axis=2, tiled=True)
    first = coulomb_tile[None] + jnp.einsum(
        "fik,kj->fij", coupled_rows, coulomb_cols, precision=HIGH
    )
    return jnp.einsum(
        "fik,fkj->fij", coupled_rows, lax.all_gather(first, "row", axis=1, tiled=True), precision=HIGH
    )


def solution(mesh):
    in_specs = (P(None, "tm"), P(None, "tm"), P("tm"), P("tm"), P(), P(), P(), P())
    out_specs = P("tm", "row", "col")
    square = mesh.shape["row"] == 4 and mesh.shape["col"] == 2

    def body(*args):
        omega, coulomb = args[6], args[7]
        fits = omega.shape[0] == 2 * mesh.shape["tm"] * mesh.shape["col"]
        fits = fits and coulomb.shape[0] % (6 * TILE) == 0 and args[0].shape[1] % 128 == 0
        return (on_plane if square and fits else on_device)(*args)

    return jax.shard_map(
        body, mesh=mesh, in_specs=in_specs, out_specs=out_specs, check_vma=False
    )
```

```python
import functools

import jax
import jax.numpy as jnp
import numpy as np
from jax import lax
from jax.experimental import pallas as pl
from jax.experimental.pallas import tpu as pltpu
from jax.sharding import PartitionSpec as P

HIGH = lax.Precision.HIGHEST
F32, BF16 = jnp.float32, jnp.bfloat16
VMEM_LIMIT = 60 << 20
TILE = 256


def halves(x):
    high = x.astype(BF16)
    return high, (x - high.astype(F32)).astype(BF16)


def dot(a, b):
    return lax.dot_general(a, b, (((1,), (0,)), ((), ())), preferred_element_type=F32)


def dot_t(a, b):
    return lax.dot_general(a, b, (((1,), (1,)), ((), ())), preferred_element_type=F32)


def dot3(a_high, a_low, b_high, b_low):
    return dot(a_high, b_high) + dot(a_low, b_high) + dot(a_high, b_low)


def split_kernel(v_ref, high_ref, low_ref):
    high_ref[...], low_ref[...] = halves(v_ref[...])


def split(v):
    rows, cols = v.shape
    spec = pl.BlockSpec((rows // 4, cols), lambda i: (i, 0))
    return pl.pallas_call(
        split_kernel,
        grid=(4,),
        in_specs=[spec],
        out_specs=[spec] * 2,
        out_shape=[jax.ShapeDtypeStruct((rows, cols), BF16)] * 2,
        compiler_params=pltpu.CompilerParams(vmem_limit_bytes=VMEM_LIMIT),
        name="split_coulomb",
    )(v)


def green_kernel(merged, first, last, meta, coef, *refs):
    refs = list(refs)
    sources = [refs.pop(0) for _ in range(merged or 2)]
    factor = refs.pop(0)
    acc_in = None if first else refs.pop(0)
    outs = [refs.pop(0) for _ in range(coef.shape[0] if last else 1)]
    c_buf, left, right, occ, sem = refs
    species, step = pl.program_id(0), pl.program_id(1)
    width = c_buf.shape[2]
    times = factor.shape[1]
    strip = left.shape[0] // times
    size = c_buf.shape[1] // 3

    def copies_of(s):
        copies = []
        for d in range(3):
            if merged:
                for k in range(d, merged, 3):
                    rows, part = sources[k].shape[1:]
                    start = pl.multiple_of(meta[k // 3 % 2], 16) + d * size
                    here = c_buf.at[s, pl.ds(start, rows), pl.ds(k // 6 * part, part)]
                    copies.append(pltpu.make_async_copy(sources[k].at[s], here, sem.at[s]))
            else:
                rows = pl.ds(pl.multiple_of(meta[2 + d], 16), size)
                here = c_buf.at[s, pl.ds(d * size, size), :]
                copies.append(pltpu.make_async_copy(sources[s].at[rows, :], here, sem.at[s]))
        return copies

    @pl.when(jnp.logical_and(species == 0, step == 0))
    def _():
        for s in range(2):
            for copy in copies_of(s):
                copy.start()

    for s in range(2):

        @pl.when(jnp.logical_and(species == s, step == 0))
        def _(s=s):
            for copy in copies_of(s):
                copy.wait()
            high, low = halves(c_buf[s])
            right[:, :width] = high
            right[:, width : 2 * width] = high
            right[:, 2 * width :] = low

    c = c_buf[species, pl.ds(pl.multiple_of(meta[5 + step], 16), strip), :]
    for t in range(times):
        high, low = halves(c * factor[species, t : t + 1, :])
        s = slice(t * strip, (t + 1) * strip)
        left[s, :width] = high
        left[s, width : 2 * width] = low
        left[s, 2 * width :] = high

    row = pl.multiple_of(meta[10 + step], 128)
    green = dot_t(left[...], right[pl.ds(row, size), :]).reshape(times, strip, size)
    if not first:
        green = green + acc_in[0, 0]
    if not last:
        outs[0][0, 0] = green
    else:

        @pl.when(species == 0)
        def _():
            occ[step] = green

        @pl.when(species == 1)
        def _():
            pairs = [occ[step, t] * green[t] for t in range(times)]
            for n, out in enumerate(outs):
                total = coef[n, 0] * pairs[0]
                for t in range(1, times):
                    total = total + coef[n, t] * pairs[t]
                out[0] = total


def green_call(name, sources, factor, meta, coef, size, acc=None, last=False):
    _, times, width = factor.shape
    strip = size // 4
    first = acc is None
    merged = 0 if first else len(sources)
    acc_spec = pl.BlockSpec((1, 1, times, strip, size), lambda s, n, *_: (s, n, 0, 0, 0))
    part_spec = pl.BlockSpec((1, strip, size), lambda s, n, *_: (s * n, 0, 0))
    args = list(sources) + [factor]
    specs = [pl.BlockSpec(memory_space=pl.ANY)] * len(sources)
    specs += [pl.BlockSpec((2, times, width), lambda s, n, *_: (0, 0, 0))]
    aliases = {}
    if not first:
        if not last:
            aliases = {2 + len(args): 0}
        args.append(acc)
        specs.append(acc_spec)
    if last:
        out_shape = [jax.ShapeDtypeStruct((5, strip, size), F32)] * coef.shape[0]
        out_specs = [part_spec] * coef.shape[0]
    else:
        out_shape = jax.ShapeDtypeStruct((2, 5, times, strip, size), F32)
        out_specs = acc_spec
    return pl.pallas_call(
        functools.partial(green_kernel, merged, first, last),
        grid_spec=pltpu.PrefetchScalarGridSpec(
            num_scalar_prefetch=2,
            grid=(2, 5),
            in_specs=specs,
            out_specs=out_specs,
            scratch_shapes=[
                pltpu.VMEM((2, 3 * size, width), F32),
                pltpu.VMEM((times * strip, 3 * width), BF16),
                pltpu.VMEM((3 * size, 3 * width), BF16),
                pltpu.VMEM((5 if last else 1, times, strip, size), F32),
                pltpu.SemaphoreType.DMA((2,)),
            ],
        ),
        out_shape=out_shape,
        input_output_aliases=aliases,
        compiler_params=pltpu.CompilerParams(vmem_limit_bytes=VMEM_LIMIT),
        cost_estimate=pl.CostEstimate(
            flops=12 * 5 * times * strip * size * width, bytes_accessed=24 << 20, transcendentals=0
        ),
        name=name,
    )(meta, coef, *args)


def chain_kernel(block, *refs):
    at, spots = refs[:2]
    parts, (v_high, v_low, near_ref, far_ref) = refs[2:10], refs[10:14]
    vh, vl, pf, ph, plo, rh, rl, xf, xh, xl, buf, sem_p, sem_v, sem_r, sem_o = refs[14:]
    n = vh.shape[0]
    m = rh.shape[0]
    half = far_ref.shape[1]
    count, strip, size = parts[0].shape
    row = pl.multiple_of(at[0], 16)
    row_copies = [
        pltpu.make_async_copy(v_high.at[pl.ds(row, m), :], rh, sem_r.at[0]),
        pltpu.make_async_copy(v_low.at[pl.ds(row, m), :], rl, sem_r.at[1]),
    ]
    p_copies = []
    for k, part in enumerate(parts):
        for t in range(count):
            i = pl.multiple_of(spots[2 * (k * count + t)], 16)
            j = pl.multiple_of(spots[2 * (k * count + t) + 1], 128)
            there = pf.at[pl.ds(i, strip), pl.ds(j, size)]
            p_copies.append(pltpu.make_async_copy(part.at[t], there, sem_p))
    v_copies = []
    for b in range(n // block):
        cols = pl.ds(b * block, block)
        v_copies.append(
            [
                pltpu.make_async_copy(v_high.at[:, cols], vh.at[:, cols], sem_v.at[0, b]),
                pltpu.make_async_copy(v_low.at[:, cols], vl.at[:, cols], sem_v.at[1, b]),
            ]
        )
    for copy in p_copies + row_copies:
        copy.start()
    for copy in p_copies + row_copies:
        copy.wait()
    for pair in v_copies:
        for copy in pair:
            copy.start()
    for b in range(n // block):
        s = slice(b * block, (b + 1) * block)
        for g in range(size, n, size):
            if s.start < g < s.stop:
                pf[g : s.stop, s.start : g] = pf[s.start : g, g : s.stop].T
        ph[: s.stop, s], plo[: s.stop, s] = halves(pf[: s.stop, s])

    def times_p(high, low, b):
        s = slice(b * block, (b + 1) * block)
        r = dot3(high[:, : s.stop], low[:, : s.stop], ph[: s.stop, s], plo[: s.stop, s])
        if s.stop < n:
            h, lo = high[:, s.stop :], low[:, s.stop :]
            ph_t, pl_t = ph[s, s.stop :], plo[s, s.stop :]
            r = r + dot_t(h, ph_t) + dot_t(lo, ph_t) + dot_t(h, pl_t)
        return r

    high, low = rh[...], rl[...]
    for b in range(n // block):
        s = slice(b * block, (b + 1) * block)
        r = times_p(high, low, b)
        xf[:, s] = r
        xh[:, s], xl[:, s] = halves(r)
    high, low = xh[...], xl[...]
    for b in range(n // block):
        for copy in v_copies[b]:
            copy.wait()
        s = slice(b * block, (b + 1) * block)
        rh[:, s], rl[:, s] = halves(dot3(high, low, vh[:, s], vl[:, s]))
    high, low = rh[...], rl[...]
    for b in range(n // block):
        s = slice(b * block, (b + 1) * block)
        xh[:, s], xl[:, s] = halves(xf[:, s] + times_p(high, low, b))
    high, low = xh[...], xl[...]
    out_copies = []
    for h in range(n // half):
        cols = slice(h * half, (h + 1) * half)
        slot = at[1] ^ h
        buf[slot] = dot3(high, low, vh[:, cols], vl[:, cols])
        for k, out in enumerate((near_ref, far_ref)):
            copy = pltpu.make_async_copy(buf.at[k], out, sem_o.at[h])

            @pl.when(slot == k)
            def _(copy=copy):
                copy.start()

        out_copies.append(copy)
    for copy in out_copies:
        copy.wait()


def chain(at, spots, parts, v_high, v_low, rows, cols):
    n = v_high.shape[0]
    block = cols
    big = pltpu.VMEM((n, n), BF16)
    strip = pltpu.VMEM((rows, n), BF16)
    smem, hbm = pl.BlockSpec(memory_space=pltpu.SMEM), pl.BlockSpec(memory_space=pl.ANY)
    scratch = [big, big, pltpu.VMEM((n, n), F32), big, big, strip, strip]
    scratch += [pltpu.VMEM((rows, n), F32), strip, strip, pltpu.VMEM((n // cols, rows, cols), F32)]
    scratch += [pltpu.SemaphoreType.DMA, pltpu.SemaphoreType.DMA((2, n // block))]
    scratch += [pltpu.SemaphoreType.DMA((2,))] * 2
    return pl.pallas_call(
        functools.partial(chain_kernel, block),
        in_specs=[smem] * 2 + [hbm] * (len(parts) + 2),
        out_specs=[hbm] * 2,
        out_shape=[jax.ShapeDtypeStruct((rows, cols), F32)] * 2,
        scratch_shapes=scratch,
        compiler_params=pltpu.CompilerParams(vmem_limit_bytes=VMEM_LIMIT),
        cost_estimate=pl.CostEstimate(
            flops=24 * rows * n * n, bytes_accessed=20 << 20, transcendentals=0
        ),
        name="chain",
    )(at, spots, *parts, v_high, v_low)


def move(v, where):
    cols = lax.axis_size("col")
    pairs = []
    for r in range(lax.axis_size("row")):
        for c in range(cols):
            x, y, core = where(c, r // 2, r % 2)
            pairs.append((r * cols + c, (2 * y + core) * cols + x))
    return lax.ppermute(v, ("row", "col"), pairs)


def over(v, dx, dy, dc):
    return move(v, lambda x, y, c: (x ^ dx, y ^ dy, c ^ dc))


def ring(v, steps=1):
    size = lax.axis_size("tm")
    return lax.ppermute(v, "tm", [(i, (i + steps) % size) for i in range(size)])


def together(*values):
    return lax.optimization_barrier(values)


def after(v, *others):
    return together(v, *others)[0]


def tables_of(size):
    strip = size // 4
    devices = [(x, y, c) for y in range(2) for c in range(2) for x in range(2)]

    def strips(x, y, c):
        return [2 * c, 2 * c + 1, 2 * x + c, 2 * y + c, 2 * x + c]

    def spots(x, y, c):
        cross = y ^ (1 - x)
        left = [2 * x + y, 2 * x + y, y, 2 * x, cross]
        right = [2 * x + y, 2 * x + y, 2 + y, 2 * x + 1, 3 - cross]
        return [(a * size + t * strip, b * size) for a, b, t in zip(left, right, strips(x, y, c))]

    meta, places = [], []
    for x, y, c in devices:
        sets = [2 * x + y, 2 * (1 - x) + y, 2 * x + 1 - y]
        left, right = [0, 0, x, 2 * y, 2 - x], [0, 0, 1 - x, 2 - 2 * y, 1 + x]
        meta.append(
            [c * 2 * strip, (1 - c) * 2 * strip]
            + [s * size for s in sets]
            + [s * size + t * strip for s, t in zip(left, strips(x, y, c))]
            + [s * size for s in right]
        )
        places.append(
            [spots(x ^ dx, y ^ dy, c ^ dc) for dc in range(2) for dx in range(2) for dy in range(2)]
        )
    flat = np.array(places, np.int32).reshape(len(devices), -1)
    return np.array(meta, np.int32), flat


def on_plane(c_occ, c_vir, eps_occ, eps_vir, tau, tweight, omega, coulomb):
    grid = coulomb.shape[0]
    planes = lax.axis_size("tm")
    rows_n, cols_n = lax.axis_size("row"), lax.axis_size("col")
    z, r, x = lax.axis_index("tm"), lax.axis_index("row"), lax.axis_index("col")
    y, core = r // 2, r % 2
    tile_rows, tile_cols = grid // rows_n, grid // cols_n
    size = grid // 4
    strip = size // 4
    ways = [(dx, dy) for dx in range(2) for dy in range(2)]
    here = (2 * y + core) * cols_n + x
    meta, spots = (jnp.array(t)[here] for t in tables_of(size))

    energies = jnp.stack([eps_occ, -eps_vir])
    arriving = [ring(energies, t) for t in range(1, planes)]

    def factor(e):
        return jnp.exp(e[None, :] * tau[:, None])

    gamma = tweight[None, :] * jnp.cos(omega[:, None] * tau[None, :])
    per_plane = omega.shape[0] // planes
    coef = -2.0 * jnp.stack(
        [gamma[z * per_plane + 2 * (x ^ dx) + (y ^ dy)] for dx, dy in ways]
    )

    start = (2 * x + y) * size + core * 2 * strip
    common = (meta, coef, size)
    piece = jnp.stack([lax.dynamic_slice_in_dim(c, start, 2 * strip, 0) for c in (c_occ, c_vir)])
    part = c_occ.shape[1]
    v_high, v_low = split(coulomb)

    def to_neighbours(v):
        return [over(v, 1, 0, 0), over(v, 0, 1, 0)]

    def with_other_core(near):
        return near + [over(v, 0, 0, 1) for v in near]

    arrived, v_high, v_low, *arriving = together(ring(piece), v_high, v_low, *arriving)
    factors = jnp.stack([factor(e) for e in jnp.concatenate(arriving, axis=1)])
    own = [after(c_occ, arrived), c_vir]
    green = green_call("green_own", own, jnp.stack([factor(e) for e in energies]), *common)
    near, sets = [arrived], []
    for t in range(2, planes):
        *near, arrived, green = together(*near, *to_neighbours(near[0]), ring(near[0]), green)
        sets.append(with_other_core(near))
        near = [arrived]
        if t == 3:
            sets[0] = list(together(*sets[0], arrived))[:-1]
    *near, green = together(
        *near,
        *to_neighbours(near[0]),
        green_call("green_first", sets[0], factors[:, :, :part], *common, green),
    )
    rest = sum(sets[1:], []) + with_other_core(near)
    parts = green_call("green_rest", rest, factors[:, :, part:], *common, green, True)

    parts = [over(p, dx, dy, 0) if dx + dy else p for p, (dx, dy) in zip(parts, ways)]
    parts += [over(p, 0, 0, 1) for p in parts]

    arrivals = []
    for e in range(2):
        at = jnp.stack([(2 * core + (y ^ e)) * tile_rows, x]).astype(jnp.int32)
        near, far = chain(at, spots, parts, v_high, v_low, tile_rows, tile_cols)
        for dx, value in ((1 - e, (near, far)[1 - e]), (e, (near, far)[e])):
            value = move(value, lambda x, y, c, dx=dx, e=e: (x ^ dx, c, y ^ e))
            arrivals.append((2 * (x ^ dx) + (core ^ e), value))
    out = jnp.zeros((per_plane, tile_rows, tile_cols), F32)
    for k, value in arrivals:
        out = lax.dynamic_update_slice(out, value[None], (k, 0, 0))
    return out


def green_block(rows_c, cols_c, energies, taus, sign):
    factor = jnp.exp(sign * taus[:, None] * energies[None, :])
    width = rows_c.shape[1]
    scaled = rows_c[:, None, :] * factor[None, :, :]
    lead = (rows_c.shape[0], taus.shape[0])
    flat = scaled.reshape(lead[0] * lead[1], width)
    product = lax.dot_general(
        flat, cols_c, (((1,), (1,)), ((), ())), precision=HIGH, preferred_element_type=F32
    )
    return product.reshape(lead[0], lead[1], cols_c.shape[0])


def on_device(c_occ, c_vir, eps_occ, eps_vir, tau, tweight, omega, coulomb):
    grid = coulomb.shape[0]
    tile_rows = grid // lax.axis_size("row")
    tile_cols = grid // lax.axis_size("col")
    row_start = lax.axis_index("row") * tile_rows
    col_start = lax.axis_index("col") * tile_cols
    occ_rows = lax.dynamic_slice_in_dim(c_occ, row_start, tile_rows, 0)
    occ_cols = lax.dynamic_slice_in_dim(c_occ, col_start, tile_cols, 0)
    vir_rows = lax.dynamic_slice_in_dim(c_vir, row_start, tile_rows, 0)
    vir_cols = lax.dynamic_slice_in_dim(c_vir, col_start, tile_cols, 0)
    gamma = tweight[None, :] * jnp.cos(omega[:, None] * tau[None, :])
    green_occ = green_block(occ_rows, occ_cols, eps_occ, tau, 1.0)
    green_vir = green_block(vir_rows, vir_cols, eps_vir, tau, -1.0)
    greens = lax.psum_scatter(
        jnp.stack([green_occ, green_vir], axis=1), "tm", scatter_dimension=0, tiled=True
    )
    polar_time = -2.0 * greens[:, 0] * greens[:, 1]
    polar_all = jnp.einsum("kj,ijc->kic", gamma, polar_time, precision=HIGH)
    polar = lax.all_to_all(polar_all, "tm", split_axis=0, concat_axis=1, tiled=True)
    coulomb_rows = lax.dynamic_slice_in_dim(coulomb, row_start, tile_rows, 0)
    coulomb_cols = lax.dynamic_slice_in_dim(coulomb, col_start, tile_cols, 1)
    coulomb_tile = lax.dynamic_slice_in_dim(coulomb_rows, col_start, tile_cols, 1)
    coupled = jnp.einsum(
        "ik,fkj->fij", coulomb_rows, lax.all_gather(polar, "row", axis=1, tiled=True), precision=HIGH
    )
    coupled_rows = lax.all_gather(coupled, "col", axis=2, tiled=True)
    first = coulomb_tile[None] + jnp.einsum(
        "fik,kj->fij", coupled_rows, coulomb_cols, precision=HIGH
    )
    return jnp.einsum(
        "fik,fkj->fij", coupled_rows, lax.all_gather(first, "row", axis=1, tiled=True), precision=HIGH
    )


def solution(mesh):
    in_specs = (P(None, "tm"), P(None, "tm"), P("tm"), P("tm"), P(), P(), P(), P())
    out_specs = P("tm", "row", "col")
    square = mesh.shape["row"] == 4 and mesh.shape["col"] == 2

    def body(*args):
        omega, coulomb = args[6], args[7]
        fits = omega.shape[0] == 2 * mesh.shape["tm"] * mesh.shape["col"]
        fits = fits and coulomb.shape[0] % (6 * TILE) == 0 and args[0].shape[1] % 128 == 0
        return (on_plane if square and fits else on_device)(*args)

    return jax.shard_map(
        body, mesh=mesh, in_specs=in_specs, out_specs=out_specs, check_vma=False
    )
```

```python
import functools

import jax
import jax.numpy as jnp
import numpy as np
from jax import lax
from jax.experimental import pallas as pl
from jax.experimental.pallas import tpu as pltpu
from jax.sharding import PartitionSpec as P

HIGH = lax.Precision.HIGHEST
F32, BF16 = jnp.float32, jnp.bfloat16
VMEM_LIMIT = 60 << 20
TILE = 256


def halves(x):
    high = x.astype(BF16)
    return high, (x - high.astype(F32)).astype(BF16)


def dot(a, b):
    return lax.dot_general(a, b, (((1,), (0,)), ((), ())), preferred_element_type=F32)


def dot_t(a, b):
    return lax.dot_general(a, b, (((1,), (1,)), ((), ())), preferred_element_type=F32)


def dot3(a_high, a_low, b_high, b_low):
    return dot(a_high, b_high) + dot(a_low, b_high) + dot(a_high, b_low)


def split_kernel(v_ref, high_ref, low_ref):
    high_ref[...], low_ref[...] = halves(v_ref[...])


def split(v):
    rows, cols = v.shape
    spec = pl.BlockSpec((rows // 4, cols), lambda i: (i, 0))
    return pl.pallas_call(
        split_kernel,
        grid=(4,),
        in_specs=[spec],
        out_specs=[spec] * 2,
        out_shape=[jax.ShapeDtypeStruct((rows, cols), BF16)] * 2,
        compiler_params=pltpu.CompilerParams(vmem_limit_bytes=VMEM_LIMIT),
        name="split_coulomb",
    )(v)


def green_kernel(merged, first, last, meta, coef, *refs):
    refs = list(refs)
    sources = [refs.pop(0) for _ in range(merged or 2)]
    factor = refs.pop(0)
    acc_in = None if first else refs.pop(0)
    outs = [refs.pop(0) for _ in range(coef.shape[0] if last else 1)]
    c_buf, left, right, occ, sem = refs
    species, step = pl.program_id(0), pl.program_id(1)
    width = c_buf.shape[2]
    times = factor.shape[1]
    strip = left.shape[0] // times
    size = c_buf.shape[1] // 3

    def copies_of(s):
        copies = []
        for d in range(3):
            if merged:
                for k in range(d, merged, 3):
                    rows, part = sources[k].shape[1:]
                    start = pl.multiple_of(meta[k // 3 % 2], 16) + d * size
                    here = c_buf.at[s, pl.ds(start, rows), pl.ds(k // 6 * part, part)]
                    copies.append(pltpu.make_async_copy(sources[k].at[s], here, sem.at[s]))
            else:
                rows = pl.ds(pl.multiple_of(meta[2 + d], 16), size)
                here = c_buf.at[s, pl.ds(d * size, size), :]
                copies.append(pltpu.make_async_copy(sources[s].at[rows, :], here, sem.at[s]))
        return copies

    @pl.when(jnp.logical_and(species == 0, step == 0))
    def _():
        for s in range(2):
            for copy in copies_of(s):
                copy.start()

    for s in range(2):

        @pl.when(jnp.logical_and(species == s, step == 0))
        def _(s=s):
            for copy in copies_of(s):
                copy.wait()
            high, low = halves(c_buf[s])
            right[:, :width] = high
            right[:, width : 2 * width] = high
            right[:, 2 * width :] = low

    c = c_buf[species, pl.ds(pl.multiple_of(meta[5 + step], 16), strip), :]
    for t in range(times):
        high, low = halves(c * factor[species, t : t + 1, :])
        s = slice(t * strip, (t + 1) * strip)
        left[s, :width] = high
        left[s, width : 2 * width] = low
        left[s, 2 * width :] = high

    row = pl.multiple_of(meta[10 + step], 128)
    green = dot_t(left[...], right[pl.ds(row, size), :]).reshape(times, strip, size)
    if not first:
        green = green + acc_in[0, 0]
    if not last:
        outs[0][0, 0] = green
    else:

        @pl.when(species == 0)
        def _():
            occ[step] = green

        @pl.when(species == 1)
        def _():
            pairs = [occ[step, t] * green[t] for t in range(times)]
            for n, out in enumerate(outs):
                total = coef[n, 0] * pairs[0]
                for t in range(1, times):
                    total = total + coef[n, t] * pairs[t]
                out[0] = total


def green_call(name, sources, factor, meta, coef, size, acc=None, last=False):
    _, times, width = factor.shape
    strip = size // 4
    first = acc is None
    merged = 0 if first else len(sources)
    acc_spec = pl.BlockSpec((1, 1, times, strip, size), lambda s, n, *_: (s, n, 0, 0, 0))
    part_spec = pl.BlockSpec((1, strip, size), lambda s, n, *_: (s * n, 0, 0))
    args = list(sources) + [factor]
    specs = [pl.BlockSpec(memory_space=pl.ANY)] * len(sources)
    specs += [pl.BlockSpec((2, times, width), lambda s, n, *_: (0, 0, 0))]
    aliases = {}
    if not first:
        if not last:
            aliases = {2 + len(args): 0}
        args.append(acc)
        specs.append(acc_spec)
    if last:
        out_shape = [jax.ShapeDtypeStruct((5, strip, size), F32)] * coef.shape[0]
        out_specs = [part_spec] * coef.shape[0]
    else:
        out_shape = jax.ShapeDtypeStruct((2, 5, times, strip, size), F32)
        out_specs = acc_spec
    return pl.pallas_call(
        functools.partial(green_kernel, merged, first, last),
        grid_spec=pltpu.PrefetchScalarGridSpec(
            num_scalar_prefetch=2,
            grid=(2, 5),
            in_specs=specs,
            out_specs=out_specs,
            scratch_shapes=[
                pltpu.VMEM((2, 3 * size, width), F32),
                pltpu.VMEM((times * strip, 3 * width), BF16),
                pltpu.VMEM((3 * size, 3 * width), BF16),
                pltpu.VMEM((5 if last else 1, times, strip, size), F32),
                pltpu.SemaphoreType.DMA((2,)),
            ],
        ),
        out_shape=out_shape,
        input_output_aliases=aliases,
        compiler_params=pltpu.CompilerParams(vmem_limit_bytes=VMEM_LIMIT),
        cost_estimate=pl.CostEstimate(
            flops=12 * 5 * times * strip * size * width, bytes_accessed=24 << 20, transcendentals=0
        ),
        name=name,
    )(meta, coef, *args)


def chain_kernel(block, *refs):
    at, spots = refs[:2]
    parts, (v_high, v_low, near_ref, far_ref) = refs[2:10], refs[10:14]
    pf, wh, wl, lh, ll, xf, sem_p, sem_v, sem_r, sem_o = refs[14:]
    n = pf.shape[0]
    m = lh.shape[1]
    blocks = n // block
    count, strip, size = parts[0].shape
    row = pl.multiple_of(at[0], 16)
    row_copies = [
        pltpu.make_async_copy(v_high.at[pl.ds(row, m), :], lh.at[0], sem_r.at[0]),
        pltpu.make_async_copy(v_low.at[pl.ds(row, m), :], ll.at[0], sem_r.at[1]),
    ]
    p_copies = []
    for k, part in enumerate(parts):
        for t in range(count):
            i = pl.multiple_of(spots[2 * (k * count + t)], 16)
            j = pl.multiple_of(spots[2 * (k * count + t) + 1], 128)
            there = pf.at[pl.ds(i, strip), pl.ds(j, size)]
            p_copies.append(pltpu.make_async_copy(part.at[t], there, sem_p))

    def v_copies(b):
        cols = pl.ds(pl.multiple_of(b * block, block), block)
        return [
            pltpu.make_async_copy(v_high.at[:, cols], wh.at[1, :, cols], sem_v.at[0, b]),
            pltpu.make_async_copy(v_low.at[:, cols], wl.at[1, :, cols], sem_v.at[1, b]),
        ]

    for copy in p_copies + row_copies:
        copy.start()
    for copy in p_copies + row_copies:
        copy.wait()
    for b in range(blocks):
        for copy in v_copies(b):
            copy.start()

    def mirror(j, _):
        def one(i, _):
            rows, cols = (pl.ds(pl.multiple_of(s * size, 128), size) for s in (i, j))
            pf[cols, rows] = pf[rows, cols].T
            return 0

        return lax.fori_loop(0, j, one, 0)

    lax.fori_loop(1, n // size, mirror, 0)

    def split_rows(i, _):
        rows = pl.ds(pl.multiple_of(i * 128, 128), 128)
        wh[0, rows], wl[0, rows] = halves(pf[rows, :])
        return 0

    lax.fori_loop(0, n // 128, split_rows, 0)

    def body(k, _):
        stage, b = lax.div(k, blocks), lax.rem(k, blocks)
        this = lax.rem(stage, 2)
        cols = pl.ds(pl.multiple_of(b * block, block), block)

        @pl.when(stage == 1)
        def _():
            for copy in v_copies(b):
                copy.wait()

        r = dot3(lh[this], ll[this], wh[this, :, cols], wl[this, :, cols])
        r = r + jnp.where(stage == 2, xf[this, :, cols], 0.0)
        xf[this, :, cols] = r
        lh[1 - this, :, cols], ll[1 - this, :, cols] = halves(r)

        @pl.when(stage == 3)
        def _():
            src = xf.at[1, :, cols]
            for out, mine in ((near_ref, True), (far_ref, False)):

                @pl.when((at[1] == b) == mine)
                def _(out=out):
                    pltpu.make_async_copy(src, out, sem_o.at[b]).start()

        return 0

    lax.fori_loop(0, 4 * blocks, body, 0)
    for h in range(blocks):
        pltpu.make_async_copy(xf.at[1, :, : block], near_ref, sem_o.at[h]).wait()


def chain(at, spots, parts, v_high, v_low, rows, cols):
    n = v_high.shape[0]
    blocks = n // cols
    smem, hbm = pl.BlockSpec(memory_space=pltpu.SMEM), pl.BlockSpec(memory_space=pl.ANY)
    scratch = [pltpu.VMEM((n, n), F32)] + [pltpu.VMEM((2, n, n), BF16)] * 2
    scratch += [pltpu.VMEM((2, rows, n), BF16)] * 2 + [pltpu.VMEM((2, rows, n), F32)]
    scratch += [pltpu.SemaphoreType.DMA, pltpu.SemaphoreType.DMA((2, blocks))]
    scratch += [pltpu.SemaphoreType.DMA((2,)), pltpu.SemaphoreType.DMA((blocks,))]
    return pl.pallas_call(
        functools.partial(chain_kernel, cols),
        in_specs=[smem] * 2 + [hbm] * (len(parts) + 2),
        out_specs=[hbm] * 2,
        out_shape=[jax.ShapeDtypeStruct((rows, cols), F32)] * 2,
        scratch_shapes=scratch,
        compiler_params=pltpu.CompilerParams(vmem_limit_bytes=VMEM_LIMIT),
        cost_estimate=pl.CostEstimate(flops=24 * rows * n * n, bytes_accessed=20 << 20, transcendentals=0),
        name="chain",
    )(at, spots, *parts, v_high, v_low)


def move(v, where):
    cols = lax.axis_size("col")
    pairs = []
    for r in range(lax.axis_size("row")):
        for c in range(cols):
            x, y, core = where(c, r // 2, r % 2)
            pairs.append((r * cols + c, (2 * y + core) * cols + x))
    return lax.ppermute(v, ("row", "col"), pairs)


def over(v, dx, dy, dc):
    return move(v, lambda x, y, c: (x ^ dx, y ^ dy, c ^ dc))


def ring(v, steps=1):
    size = lax.axis_size("tm")
    return lax.ppermute(v, "tm", [(i, (i + steps) % size) for i in range(size)])


def together(*values):
    return lax.optimization_barrier(values)


def after(v, *others):
    return together(v, *others)[0]


def tables_of(size):
    strip = size // 4
    devices = [(x, y, c) for y in range(2) for c in range(2) for x in range(2)]

    def strips(x, y, c):
        return [2 * c, 2 * c + 1, 2 * x + c, 2 * y + c, 2 * x + c]

    def spots(x, y, c):
        cross = y ^ (1 - x)
        left = [2 * x + y, 2 * x + y, y, 2 * x, cross]
        right = [2 * x + y, 2 * x + y, 2 + y, 2 * x + 1, 3 - cross]
        return [(a * size + t * strip, b * size) for a, b, t in zip(left, right, strips(x, y, c))]

    meta, places = [], []
    for x, y, c in devices:
        sets = [2 * x + y, 2 * (1 - x) + y, 2 * x + 1 - y]
        left, right = [0, 0, x, 2 * y, 2 - x], [0, 0, 1 - x, 2 - 2 * y, 1 + x]
        meta.append(
            [c * 2 * strip, (1 - c) * 2 * strip]
            + [s * size for s in sets]
            + [s * size + t * strip for s, t in zip(left, strips(x, y, c))]
            + [s * size for s in right]
        )
        places.append(
            [spots(x ^ dx, y ^ dy, c ^ dc) for dc in range(2) for dx in range(2) for dy in range(2)]
        )
    flat = np.array(places, np.int32).reshape(len(devices), -1)
    return np.array(meta, np.int32), flat


def on_plane(c_occ, c_vir, eps_occ, eps_vir, tau, tweight, omega, coulomb):
    grid = coulomb.shape[0]
    planes = lax.axis_size("tm")
    rows_n, cols_n = lax.axis_size("row"), lax.axis_size("col")
    z, r, x = lax.axis_index("tm"), lax.axis_index("row"), lax.axis_index("col")
    y, core = r // 2, r % 2
    tile_rows, tile_cols = grid // rows_n, grid // cols_n
    size = grid // 4
    strip = size // 4
    ways = [(dx, dy) for dx in range(2) for dy in range(2)]
    here = (2 * y + core) * cols_n + x
    meta, spots = (jnp.array(t)[here] for t in tables_of(size))

    energies = jnp.stack([eps_occ, -eps_vir])
    arriving = [ring(energies, t) for t in range(1, planes)]

    def factor(e):
        return jnp.exp(e[None, :] * tau[:, None])

    gamma = tweight[None, :] * jnp.cos(omega[:, None] * tau[None, :])
    per_plane = omega.shape[0] // planes
    coef = -2.0 * jnp.stack(
        [gamma[z * per_plane + 2 * (x ^ dx) + (y ^ dy)] for dx, dy in ways]
    )

    start = (2 * x + y) * size + core * 2 * strip
    common = (meta, coef, size)
    piece = jnp.stack([lax.dynamic_slice_in_dim(c, start, 2 * strip, 0) for c in (c_occ, c_vir)])
    part = c_occ.shape[1]
    v_high, v_low = split(coulomb)

    def to_neighbours(v):
        return [over(v, 1, 0, 0), over(v, 0, 1, 0)]

    def with_other_core(near):
        return near + [over(v, 0, 0, 1) for v in near]

    arrived, v_high, v_low, *arriving = together(ring(piece), v_high, v_low, *arriving)
    factors = jnp.stack([factor(e) for e in jnp.concatenate(arriving, axis=1)])
    own = [after(c_occ, arrived), c_vir]
    green = green_call("green_own", own, jnp.stack([factor(e) for e in energies]), *common)
    near, sets = [arrived], []
    for t in range(2, planes):
        *near, arrived, green = together(*near, *to_neighbours(near[0]), ring(near[0]), green)
        sets.append(with_other_core(near))
        near = [arrived]
        if t == 3:
            sets[0] = list(together(*sets[0], arrived))[:-1]
    *near, green = together(
        *near,
        *to_neighbours(near[0]),
        green_call("green_first", sets[0], factors[:, :, :part], *common, green),
    )
    rest = sum(sets[1:], []) + with_other_core(near)
    parts = green_call("green_rest", rest, factors[:, :, part:], *common, green, True)

    parts = [over(p, dx, dy, 0) if dx + dy else p for p, (dx, dy) in zip(parts, ways)]
    parts += [over(p, 0, 0, 1) for p in parts]

    arrivals = []
    for e in range(2):
        at = jnp.stack([(2 * core + (y ^ e)) * tile_rows, x]).astype(jnp.int32)
        near, far = chain(at, spots, parts, v_high, v_low, tile_rows, tile_cols)
        for dx, value in ((1 - e, (near, far)[1 - e]), (e, (near, far)[e])):
            value = move(value, lambda x, y, c, dx=dx, e=e: (x ^ dx, c, y ^ e))
            arrivals.append((2 * (x ^ dx) + (core ^ e), value))
    out = jnp.zeros((per_plane, tile_rows, tile_cols), F32)
    for k, value in arrivals:
        out = lax.dynamic_update_slice(out, value[None], (k, 0, 0))
    return out


def green_block(rows_c, cols_c, energies, taus, sign):
    factor = jnp.exp(sign * taus[:, None] * energies[None, :])
    width = rows_c.shape[1]
    scaled = rows_c[:, None, :] * factor[None, :, :]
    lead = (rows_c.shape[0], taus.shape[0])
    flat = scaled.reshape(lead[0] * lead[1], width)
    product = lax.dot_general(
        flat, cols_c, (((1,), (1,)), ((), ())), precision=HIGH, preferred_element_type=F32
    )
    return product.reshape(lead[0], lead[1], cols_c.shape[0])


def on_device(c_occ, c_vir, eps_occ, eps_vir, tau, tweight, omega, coulomb):
    grid = coulomb.shape[0]
    tile_rows = grid // lax.axis_size("row")
    tile_cols = grid // lax.axis_size("col")
    row_start = lax.axis_index("row") * tile_rows
    col_start = lax.axis_index("col") * tile_cols
    occ_rows = lax.dynamic_slice_in_dim(c_occ, row_start, tile_rows, 0)
    occ_cols = lax.dynamic_slice_in_dim(c_occ, col_start, tile_cols, 0)
    vir_rows = lax.dynamic_slice_in_dim(c_vir, row_start, tile_rows, 0)
    vir_cols = lax.dynamic_slice_in_dim(c_vir, col_start, tile_cols, 0)
    gamma = tweight[None, :] * jnp.cos(omega[:, None] * tau[None, :])
    green_occ = green_block(occ_rows, occ_cols, eps_occ, tau, 1.0)
    green_vir = green_block(vir_rows, vir_cols, eps_vir, tau, -1.0)
    greens = lax.psum_scatter(
        jnp.stack([green_occ, green_vir], axis=1), "tm", scatter_dimension=0, tiled=True
    )
    polar_time = -2.0 * greens[:, 0] * greens[:, 1]
    polar_all = jnp.einsum("kj,ijc->kic", gamma, polar_time, precision=HIGH)
    polar = lax.all_to_all(polar_all, "tm", split_axis=0, concat_axis=1, tiled=True)
    coulomb_rows = lax.dynamic_slice_in_dim(coulomb, row_start, tile_rows, 0)
    coulomb_cols = lax.dynamic_slice_in_dim(coulomb, col_start, tile_cols, 1)
    coulomb_tile = lax.dynamic_slice_in_dim(coulomb_rows, col_start, tile_cols, 1)
    coupled = jnp.einsum(
        "ik,fkj->fij", coulomb_rows, lax.all_gather(polar, "row", axis=1, tiled=True), precision=HIGH
    )
    coupled_rows = lax.all_gather(coupled, "col", axis=2, tiled=True)
    first = coulomb_tile[None] + jnp.einsum(
        "fik,kj->fij", coupled_rows, coulomb_cols, precision=HIGH
    )
    return jnp.einsum(
        "fik,fkj->fij", coupled_rows, lax.all_gather(first, "row", axis=1, tiled=True), precision=HIGH
    )


def solution(mesh):
    in_specs = (P(None, "tm"), P(None, "tm"), P("tm"), P("tm"), P(), P(), P(), P())
    out_specs = P("tm", "row", "col")
    square = mesh.shape["row"] == 4 and mesh.shape["col"] == 2

    def body(*args):
        omega, coulomb = args[6], args[7]
        fits = omega.shape[0] == 2 * mesh.shape["tm"] * mesh.shape["col"]
        fits = fits and coulomb.shape[0] % (6 * TILE) == 0 and args[0].shape[1] % 128 == 0
        return (on_plane if square and fits else on_device)(*args)

    return jax.shard_map(
        body, mesh=mesh, in_specs=in_specs, out_specs=out_specs, check_vma=False
    )
```

```python
import functools

import jax
import jax.numpy as jnp
import numpy as np
from jax import lax
from jax.experimental import pallas as pl
from jax.experimental.pallas import tpu as pltpu
from jax.sharding import PartitionSpec as P

HIGH = lax.Precision.HIGHEST
F32, BF16 = jnp.float32, jnp.bfloat16
VMEM_LIMIT = 60 << 20
TILE = 256
SOME = 2


def halves(x):
    high = x.astype(BF16)
    return high, (x - high.astype(F32)).astype(BF16)


def dot(a, b):
    return lax.dot_general(a, b, (((1,), (0,)), ((), ())), preferred_element_type=F32)


def dot_t(a, b):
    return lax.dot_general(a, b, (((1,), (1,)), ((), ())), preferred_element_type=F32)


def dot3(a_high, a_low, b_high, b_low):
    return dot(a_high, b_high) + dot(a_low, b_high) + dot(a_high, b_low)


def split_kernel(v_ref, high_ref, low_ref):
    high_ref[...], low_ref[...] = halves(v_ref[...])


def split(v):
    rows, cols = v.shape
    spec = pl.BlockSpec((rows // 4, cols), lambda i: (i, 0))
    return pl.pallas_call(
        split_kernel,
        grid=(4,),
        in_specs=[spec],
        out_specs=[spec] * 2,
        out_shape=[jax.ShapeDtypeStruct((rows, cols), BF16)] * 2,
        compiler_params=pltpu.CompilerParams(vmem_limit_bytes=VMEM_LIMIT),
        name="split_coulomb",
    )(v)


def green_kernel(merged, first, last, step0, meta, coef, *refs):
    refs = list(refs)
    sources = [refs.pop(0) for _ in range(merged or 2)]
    factor = refs.pop(0)
    acc_in = None if first else refs.pop(0)
    outs = [refs.pop(0) for _ in range(coef.shape[0] if last else 1)]
    c_buf, left, right, occ, sem = refs
    species, here = pl.program_id(0), pl.program_id(1)
    step = here + step0
    width = c_buf.shape[2]
    times = factor.shape[1]
    strip = left.shape[0] // times
    size = c_buf.shape[1] // 3

    def copies_of(s):
        copies = []
        for d in range(3):
            if merged:
                for k in range(d, merged, 3):
                    rows, part = sources[k].shape[1:]
                    start = pl.multiple_of(meta[k // 3 % 2], 16) + d * size
                    there = c_buf.at[s, pl.ds(start, rows), pl.ds(k // 6 * part, part)]
                    copies.append(pltpu.make_async_copy(sources[k].at[s], there, sem.at[s]))
            else:
                rows = pl.ds(pl.multiple_of(meta[2 + d], 16), size)
                there = c_buf.at[s, pl.ds(d * size, size), :]
                copies.append(pltpu.make_async_copy(sources[s].at[rows, :], there, sem.at[s]))
        return copies

    @pl.when(jnp.logical_and(species == 0, here == 0))
    def _():
        for s in range(2):
            for copy in copies_of(s):
                copy.start()

    for s in range(2):

        @pl.when(jnp.logical_and(species == s, here == 0))
        def _(s=s):
            for copy in copies_of(s):
                copy.wait()
            high, low = halves(c_buf[s])
            right[:, :width] = high
            right[:, width : 2 * width] = high
            right[:, 2 * width :] = low

    c = c_buf[species, pl.ds(pl.multiple_of(meta[5 + step], 16), strip), :]
    for t in range(times):
        high, low = halves(c * factor[species, t : t + 1, :])
        s = slice(t * strip, (t + 1) * strip)
        left[s, :width] = high
        left[s, width : 2 * width] = low
        left[s, 2 * width :] = high

    row = pl.multiple_of(meta[10 + step], 128)
    green = dot_t(left[...], right[pl.ds(row, size), :]).reshape(times, strip, size)
    if not first:
        green = green + acc_in[0, 0]
    if not last:
        outs[0][0, 0] = green
    else:

        @pl.when(species == 0)
        def _():
            occ[here] = green

        @pl.when(species == 1)
        def _():
            pairs = [occ[here, t] * green[t] for t in range(times)]
            for n, out in enumerate(outs):
                total = coef[n, 0] * pairs[0]
                for t in range(1, times):
                    total = total + coef[n, t] * pairs[t]
                out[0] = total


def green_call(name, sources, factor, meta, coef, size, acc=None, last=False, strips=range(5)):
    _, times, width = factor.shape
    strip = size // 4
    first = acc is None
    merged = 0 if first else len(sources)
    n0 = strips[0]
    acc_spec = pl.BlockSpec((1, 1, times, strip, size), lambda s, n, *_: (s, n + n0, 0, 0, 0))
    part_spec = pl.BlockSpec((1, strip, size), lambda s, n, *_: (s * n, 0, 0))
    args = list(sources) + [factor]
    specs = [pl.BlockSpec(memory_space=pl.ANY)] * len(sources)
    specs += [pl.BlockSpec((2, times, width), lambda s, n, *_: (0, 0, 0))]
    aliases = {}
    if not first:
        if not last:
            aliases = {2 + len(args): 0}
        args.append(acc)
        specs.append(acc_spec)
    if last:
        out_shape = [jax.ShapeDtypeStruct((len(strips), strip, size), F32)] * coef.shape[0]
        out_specs = [part_spec] * coef.shape[0]
    else:
        out_shape = jax.ShapeDtypeStruct((2, 5, times, strip, size), F32)
        out_specs = acc_spec
    return pl.pallas_call(
        functools.partial(green_kernel, merged, first, last, n0),
        grid_spec=pltpu.PrefetchScalarGridSpec(
            num_scalar_prefetch=2,
            grid=(2, len(strips)),
            in_specs=specs,
            out_specs=out_specs,
            scratch_shapes=[
                pltpu.VMEM((2, 3 * size, width), F32),
                pltpu.VMEM((times * strip, 3 * width), BF16),
                pltpu.VMEM((3 * size, 3 * width), BF16),
                pltpu.VMEM((len(strips) if last else 1, times, strip, size), F32),
                pltpu.SemaphoreType.DMA((2,)),
            ],
        ),
        out_shape=out_shape,
        input_output_aliases=aliases,
        compiler_params=pltpu.CompilerParams(vmem_limit_bytes=VMEM_LIMIT),
        cost_estimate=pl.CostEstimate(
            flops=12 * 5 * times * strip * size * width, bytes_accessed=24 << 20, transcendentals=0
        ),
        name=name,
    )(meta, coef, *args)


def chain_kernel(block, *refs):
    at, spots = refs[:2]
    parts, (v_high, v_low, near_ref, far_ref) = refs[2:-14], refs[-14:-10]
    pf, wh, wl, lh, ll, xf, sem_p, sem_v, sem_r, sem_o = refs[-10:]
    n = pf.shape[0]
    m = lh.shape[1]
    blocks = n // block
    size = parts[0].shape[2]
    row = pl.multiple_of(at[0], 16)
    row_copies = [
        pltpu.make_async_copy(v_high.at[pl.ds(row, m), :], lh.at[0], sem_r.at[0]),
        pltpu.make_async_copy(v_low.at[pl.ds(row, m), :], ll.at[0], sem_r.at[1]),
    ]
    p_copies = []
    for part in parts:
        for t in range(part.shape[0]):
            k = len(p_copies)
            i = pl.multiple_of(spots[2 * k], 16)
            j = pl.multiple_of(spots[2 * k + 1], 128)
            there = pf.at[pl.ds(i, part.shape[1]), pl.ds(j, size)]
            p_copies.append(pltpu.make_async_copy(part.at[t], there, sem_p))

    def v_copies(b):
        cols = pl.ds(pl.multiple_of(b * block, block), block)
        return [
            pltpu.make_async_copy(v_high.at[:, cols], wh.at[1, :, cols], sem_v.at[0, b]),
            pltpu.make_async_copy(v_low.at[:, cols], wl.at[1, :, cols], sem_v.at[1, b]),
        ]

    for copy in p_copies + row_copies:
        copy.start()
    for copy in p_copies:
        copy.wait()
    for b in range(blocks):
        for copy in v_copies(b):
            copy.start()

    def mirror(j, _):
        def one(i, _):
            rows, cols = (pl.ds(pl.multiple_of(s * size, 128), size) for s in (i, j))
            pf[cols, rows] = pf[rows, cols].T
            return 0

        return lax.fori_loop(0, j, one, 0)

    lax.fori_loop(1, n // size, mirror, 0)

    def split_rows(i, _):
        rows = pl.ds(pl.multiple_of(i * 128, 128), 128)
        wh[0, rows], wl[0, rows] = halves(pf[rows, :])
        return 0

    lax.fori_loop(0, n // 128, split_rows, 0)

    for copy in row_copies:
        copy.wait()

    def body(k, _):
        stage, b = lax.div(k, blocks), lax.rem(k, blocks)
        this = lax.rem(stage, 2)
        cols = pl.ds(pl.multiple_of(b * block, block), block)

        @pl.when(stage == 1)
        def _():
            for copy in v_copies(b):
                copy.wait()

        r = dot3(lh[this], ll[this], wh[this, :, cols], wl[this, :, cols])
        r = r + jnp.where(stage == 2, xf[this, :, cols], 0.0)
        xf[this, :, cols] = r
        lh[1 - this, :, cols], ll[1 - this, :, cols] = halves(r)

        @pl.when(stage == 3)
        def _():
            src = xf.at[1, :, cols]
            for out, mine in ((near_ref, True), (far_ref, False)):

                @pl.when((at[1] == b) == mine)
                def _(out=out):
                    pltpu.make_async_copy(src, out, sem_o.at[b]).start()

        return 0

    lax.fori_loop(0, 4 * blocks, body, 0)
    for h in range(blocks):
        pltpu.make_async_copy(xf.at[1, :, : block], near_ref, sem_o.at[h]).wait()


def chain(at, spots, parts, v_high, v_low, rows, cols):
    n = v_high.shape[0]
    blocks = n // cols
    smem, hbm = pl.BlockSpec(memory_space=pltpu.SMEM), pl.BlockSpec(memory_space=pl.ANY)
    scratch = [pltpu.VMEM((n, n), F32)] + [pltpu.VMEM((2, n, n), BF16)] * 2
    scratch += [pltpu.VMEM((2, rows, n), BF16)] * 2 + [pltpu.VMEM((2, rows, n), F32)]
    scratch += [pltpu.SemaphoreType.DMA, pltpu.SemaphoreType.DMA((2, blocks))]
    scratch += [pltpu.SemaphoreType.DMA((2,)), pltpu.SemaphoreType.DMA((blocks,))]
    return pl.pallas_call(
        functools.partial(chain_kernel, cols),
        in_specs=[smem] * 2 + [hbm] * (len(parts) + 2),
        out_specs=[hbm] * 2,
        out_shape=[jax.ShapeDtypeStruct((rows, cols), F32)] * 2,
        scratch_shapes=scratch,
        compiler_params=pltpu.CompilerParams(vmem_limit_bytes=VMEM_LIMIT),
        cost_estimate=pl.CostEstimate(flops=24 * rows * n * n, bytes_accessed=20 << 20, transcendentals=0),
        name="chain",
    )(at, spots, *parts, v_high, v_low)


def move(v, where):
    cols = lax.axis_size("col")
    pairs = []
    for r in range(lax.axis_size("row")):
        for c in range(cols):
            x, y, core = where(c, r // 2, r % 2)
            pairs.append((r * cols + c, (2 * y + core) * cols + x))
    return lax.ppermute(v, ("row", "col"), pairs)


def over(v, dx, dy, dc):
    return move(v, lambda x, y, c: (x ^ dx, y ^ dy, c ^ dc))


def ring(v, steps=1):
    size = lax.axis_size("tm")
    return lax.ppermute(v, "tm", [(i, (i + steps) % size) for i in range(size)])


def together(*values):
    return lax.optimization_barrier(values)


def after(v, *others):
    return together(v, *others)[0]


def tables_of(size, tile_rows):
    strip = size // 4
    devices = [(x, y, c) for y in range(2) for c in range(2) for x in range(2)]

    def strips(x, y, c):
        return [2 * c, 2 * c + 1, 2 * x + c, 2 * y + c, 2 * x + c]

    def spots(x, y, c):
        cross = y ^ (1 - x)
        left = [2 * x + y, y, 2 * x, cross]
        right = [2 * x + y, 2 + y, 2 * x + 1, 3 - cross]
        return [(a * size + t * strip, b * size) for a, b, t in zip(left, right, strips(x, y, c)[:1] + strips(x, y, c)[2:])]

    meta, places, at = [], [], []
    for x, y, c in devices:
        sets = [2 * x + y, 2 * (1 - x) + y, 2 * x + 1 - y]
        left, right = [0, 0, x, 2 * y, 2 - x], [0, 0, 1 - x, 2 - 2 * y, 1 + x]
        meta.append(
            [c * 2 * strip, (1 - c) * 2 * strip]
            + [s * size for s in sets]
            + [s * size + t * strip for s, t in zip(left, strips(x, y, c))]
            + [s * size for s in right]
        )
        at.append([[(2 * c + (y ^ e)) * tile_rows, x] for e in range(2)])
        places.append(
            [spots(x ^ dx, y ^ dy, c ^ dc) for dc in range(2) for dx in range(2) for dy in range(2)]
        )
    flat = np.array(places, np.int32).reshape(len(devices), -1)
    return np.array(meta, np.int32), flat, np.array(at, np.int32)


def on_plane(c_occ, c_vir, eps_occ, eps_vir, tau, tweight, omega, coulomb):
    grid = coulomb.shape[0]
    planes = lax.axis_size("tm")
    rows_n, cols_n = lax.axis_size("row"), lax.axis_size("col")
    z, r, x = lax.axis_index("tm"), lax.axis_index("row"), lax.axis_index("col")
    y, core = r // 2, r % 2
    tile_rows, tile_cols = grid // rows_n, grid // cols_n
    size = grid // 4
    strip = size // 4
    ways = [(dx, dy) for dx in range(2) for dy in range(2)]
    here = (2 * y + core) * cols_n + x
    meta_of, spots_of, at_of = tables_of(size, tile_rows)
    meta = jnp.array(meta_of)[here]

    energies = jnp.stack([eps_occ, -eps_vir])
    arriving = [ring(energies, t) for t in range(1, planes)]

    def factor(e):
        return jnp.exp(e[None, :] * tau[:, None])

    gamma = tweight[None, :] * jnp.cos(omega[:, None] * tau[None, :])
    per_plane = omega.shape[0] // planes
    coef = -2.0 * jnp.stack(
        [gamma[z * per_plane + 2 * (x ^ dx) + (y ^ dy)] for dx, dy in ways]
    )

    start = (2 * x + y) * size + core * 2 * strip
    common = (meta, coef, size)
    piece = jnp.stack([lax.dynamic_slice_in_dim(c, start, 2 * strip, 0) for c in (c_occ, c_vir)])
    part = c_occ.shape[1]
    v_high, v_low = split(coulomb)

    def to_neighbours(v):
        return [over(v, 1, 0, 0), over(v, 0, 1, 0)]

    def with_other_core(near):
        return near + [over(v, 0, 0, 1) for v in near]

    arrived, v_high, v_low, *arriving = together(ring(piece), v_high, v_low, *arriving)
    factors = jnp.stack([factor(e) for e in jnp.concatenate(arriving, axis=1)])
    own = [after(c_occ, arrived), c_vir]
    green = green_call("green_own", own, jnp.stack([factor(e) for e in energies]), *common)
    near, sets = [arrived], []
    for t in range(2, planes):
        *near, arrived, green = together(*near, *to_neighbours(near[0]), ring(near[0]), green)
        sets.append(with_other_core(near))
        near = [arrived]
        if t == 3:
            sets[0] = list(together(*sets[0], arrived))[:-1]
    *near, green = together(
        *near,
        *to_neighbours(near[0]),
        green_call("green_first", sets[0], factors[:, :, :part], *common, green),
    )
    rest = sum(sets[1:], []) + with_other_core(near)
    rest = functools.partial(green_call, "green_rest", rest, factors[:, :, part:], *common)

    def to_chips(parts):
        return [over(p, dx, dy, 0) if dx + dy else p for p, (dx, dy) in zip(parts, ways)]

    some = rest(green, True, range(SOME))
    more = rest(after(green, *some), True, range(SOME, 5))
    both = together(*to_chips(some), *more)
    some, more = both[: len(ways)], both[len(ways) :]
    here, _ = together(here, more[0])
    spots, at = jnp.array(spots_of)[here], jnp.array(at_of)[here]
    more, spots, at = together(to_chips(more), spots, at)
    some = [p.reshape(1, SOME * strip, size) for p in some]
    parts = [p for pair in zip(some, more) for p in pair]
    parts += [over(p, 0, 0, 1) for p in parts]

    arrivals = []
    for e in range(2):
        near, far = chain(at[e], spots, parts, v_high, v_low, tile_rows, tile_cols)
        for dx, value in ((1 - e, (near, far)[1 - e]), (e, (near, far)[e])):
            value = move(value, lambda x, y, c, dx=dx, e=e: (x ^ dx, c, y ^ e))
            arrivals.append((2 * (x ^ dx) + (core ^ e), value))
    out = jnp.zeros((per_plane, tile_rows, tile_cols), F32)
    for k, value in arrivals:
        out = lax.dynamic_update_slice(out, value[None], (k, 0, 0))
    return out


def green_block(rows_c, cols_c, energies, taus, sign):
    factor = jnp.exp(sign * taus[:, None] * energies[None, :])
    width = rows_c.shape[1]
    scaled = rows_c[:, None, :] * factor[None, :, :]
    lead = (rows_c.shape[0], taus.shape[0])
    flat = scaled.reshape(lead[0] * lead[1], width)
    product = lax.dot_general(
        flat, cols_c, (((1,), (1,)), ((), ())), precision=HIGH, preferred_element_type=F32
    )
    return product.reshape(lead[0], lead[1], cols_c.shape[0])


def on_device(c_occ, c_vir, eps_occ, eps_vir, tau, tweight, omega, coulomb):
    grid = coulomb.shape[0]
    tile_rows = grid // lax.axis_size("row")
    tile_cols = grid // lax.axis_size("col")
    row_start = lax.axis_index("row") * tile_rows
    col_start = lax.axis_index("col") * tile_cols
    occ_rows = lax.dynamic_slice_in_dim(c_occ, row_start, tile_rows, 0)
    occ_cols = lax.dynamic_slice_in_dim(c_occ, col_start, tile_cols, 0)
    vir_rows = lax.dynamic_slice_in_dim(c_vir, row_start, tile_rows, 0)
    vir_cols = lax.dynamic_slice_in_dim(c_vir, col_start, tile_cols, 0)
    gamma = tweight[None, :] * jnp.cos(omega[:, None] * tau[None, :])
    green_occ = green_block(occ_rows, occ_cols, eps_occ, tau, 1.0)
    green_vir = green_block(vir_rows, vir_cols, eps_vir, tau, -1.0)
    greens = lax.psum_scatter(
        jnp.stack([green_occ, green_vir], axis=1), "tm", scatter_dimension=0, tiled=True
    )
    polar_time = -2.0 * greens[:, 0] * greens[:, 1]
    polar_all = jnp.einsum("kj,ijc->kic", gamma, polar_time, precision=HIGH)
    polar = lax.all_to_all(polar_all, "tm", split_axis=0, concat_axis=1, tiled=True)
    coulomb_rows = lax.dynamic_slice_in_dim(coulomb, row_start, tile_rows, 0)
    coulomb_cols = lax.dynamic_slice_in_dim(coulomb, col_start, tile_cols, 1)
    coulomb_tile = lax.dynamic_slice_in_dim(coulomb_rows, col_start, tile_cols, 1)
    coupled = jnp.einsum(
        "ik,fkj->fij", coulomb_rows, lax.all_gather(polar, "row", axis=1, tiled=True), precision=HIGH
    )
    coupled_rows = lax.all_gather(coupled, "col", axis=2, tiled=True)
    first = coulomb_tile[None] + jnp.einsum(
        "fik,kj->fij", coupled_rows, coulomb_cols, precision=HIGH
    )
    return jnp.einsum(
        "fik,fkj->fij", coupled_rows, lax.all_gather(first, "row", axis=1, tiled=True), precision=HIGH
    )


def solution(mesh):
    in_specs = (P(None, "tm"), P(None, "tm"), P("tm"), P("tm"), P(), P(), P(), P())
    out_specs = P("tm", "row", "col")
    square = mesh.shape["row"] == 4 and mesh.shape["col"] == 2

    def body(*args):
        omega, coulomb = args[6], args[7]
        fits = omega.shape[0] == 2 * mesh.shape["tm"] * mesh.shape["col"]
        fits = fits and coulomb.shape[0] % (6 * TILE) == 0 and args[0].shape[1] % 128 == 0
        return (on_plane if square and fits else on_device)(*args)

    return jax.shard_map(
        body, mesh=mesh, in_specs=in_specs, out_specs=out_specs, check_vma=False
    )
```

```python
import functools

import jax
import jax.numpy as jnp
import numpy as np
from jax import lax
from jax.experimental import pallas as pl
from jax.experimental.pallas import tpu as pltpu
from jax.sharding import PartitionSpec as P

HIGH = lax.Precision.HIGHEST
F32, BF16 = jnp.float32, jnp.bfloat16
VMEM_LIMIT = 60 << 20
TILE = 256
SOME = 2


def halves(x):
    high = x.astype(BF16)
    return high, (x - high.astype(F32)).astype(BF16)


def dot(a, b):
    return lax.dot_general(a, b, (((1,), (0,)), ((), ())), preferred_element_type=F32)


def dot_t(a, b):
    return lax.dot_general(a, b, (((1,), (1,)), ((), ())), preferred_element_type=F32)


def dot3(a_high, a_low, b_high, b_low):
    return dot(a_high, b_high) + dot(a_low, b_high) + dot(a_high, b_low)


def split_kernel(v_ref, high_ref, low_ref):
    high_ref[...], low_ref[...] = halves(v_ref[...])


def split(v):
    rows, cols = v.shape
    spec = pl.BlockSpec((rows // 4, cols), lambda i: (i, 0))
    return pl.pallas_call(
        split_kernel,
        grid=(4,),
        in_specs=[spec],
        out_specs=[spec] * 2,
        out_shape=[jax.ShapeDtypeStruct((rows, cols), BF16)] * 2,
        compiler_params=pltpu.CompilerParams(vmem_limit_bytes=VMEM_LIMIT),
        name="split_coulomb",
    )(v)


def green_kernel(merged, first, last, step0, meta, coef, *refs):
    refs = list(refs)
    sources = [refs.pop(0) for _ in range(merged or 2)]
    factor = refs.pop(0)
    acc_in = None if first else refs.pop(0)
    outs = [refs.pop(0) for _ in range(coef.shape[0] if last else 1)]
    c_buf, left, right, occ, sem = refs
    species, here = pl.program_id(0), pl.program_id(1)
    step = here + step0
    width = c_buf.shape[2]
    times = factor.shape[1]
    strip = left.shape[0] // times
    size = c_buf.shape[1] // 3

    def copies_of(s):
        copies = []
        for d in range(3):
            if merged:
                for k in range(d, merged, 3):
                    rows, part = sources[k].shape[1:]
                    start = pl.multiple_of(meta[k // 3 % 2], 16) + d * size
                    there = c_buf.at[s, pl.ds(start, rows), pl.ds(k // 6 * part, part)]
                    copies.append(pltpu.make_async_copy(sources[k].at[s], there, sem.at[s]))
            else:
                rows = pl.ds(pl.multiple_of(meta[2 + d], 16), size)
                there = c_buf.at[s, pl.ds(d * size, size), :]
                copies.append(pltpu.make_async_copy(sources[s].at[rows, :], there, sem.at[s]))
        return copies

    for s in range(2):

        @pl.when(jnp.logical_and(species == s, here == 0))
        def _(s=s):
            if s == 0:
                for copy in copies_of(0):
                    copy.start()
            for copy in copies_of(s):
                copy.wait()
            if s == 0:
                for copy in copies_of(1):
                    copy.start()
            high, low = halves(c_buf[s])
            right[:, :width] = high
            right[:, width : 2 * width] = high
            right[:, 2 * width :] = low

    c = c_buf[species, pl.ds(pl.multiple_of(meta[5 + step], 16), strip), :]
    for t in range(times):
        high, low = halves(c * factor[species, t : t + 1, :])
        s = slice(t * strip, (t + 1) * strip)
        left[s, :width] = high
        left[s, width : 2 * width] = low
        left[s, 2 * width :] = high

    row = pl.multiple_of(meta[10 + step], 128)
    green = dot_t(left[...], right[pl.ds(row, size), :]).reshape(times, strip, size)
    if not first:
        green = green + acc_in[0, 0]
    if not last:
        outs[0][0, 0] = green
    else:

        @pl.when(species == 0)
        def _():
            occ[here] = green

        @pl.when(species == 1)
        def _():
            pairs = [occ[here, t] * green[t] for t in range(times)]
            for n, out in enumerate(outs):
                total = coef[n, 0] * pairs[0]
                for t in range(1, times):
                    total = total + coef[n, t] * pairs[t]
                out[0] = total


def green_call(name, sources, factor, meta, coef, size, acc=None, last=False, strips=range(5)):
    _, times, width = factor.shape
    strip = size // 4
    first = acc is None
    merged = 0 if first else len(sources)
    n0 = strips[0]
    acc_spec = pl.BlockSpec((1, 1, times, strip, size), lambda s, n, *_: (s, n + n0, 0, 0, 0))
    part_spec = pl.BlockSpec((1, strip, size), lambda s, n, *_: (s * n, 0, 0))
    args = list(sources) + [factor]
    specs = [pl.BlockSpec(memory_space=pl.ANY)] * len(sources)
    specs += [pl.BlockSpec((2, times, width), lambda s, n, *_: (0, 0, 0))]
    aliases = {}
    if not first:
        if not last:
            aliases = {2 + len(args): 0}
        args.append(acc)
        specs.append(acc_spec)
    if last:
        out_shape = [jax.ShapeDtypeStruct((len(strips), strip, size), F32)] * coef.shape[0]
        out_specs = [part_spec] * coef.shape[0]
    else:
        out_shape = jax.ShapeDtypeStruct((2, 5, times, strip, size), F32)
        out_specs = acc_spec
    return pl.pallas_call(
        functools.partial(green_kernel, merged, first, last, n0),
        grid_spec=pltpu.PrefetchScalarGridSpec(
            num_scalar_prefetch=2,
            grid=(2, len(strips)),
            in_specs=specs,
            out_specs=out_specs,
            scratch_shapes=[
                pltpu.VMEM((2, 3 * size, width), F32),
                pltpu.VMEM((times * strip, 3 * width), BF16),
                pltpu.VMEM((3 * size, 3 * width), BF16),
                pltpu.VMEM((len(strips) if last else 1, times, strip, size), F32),
                pltpu.SemaphoreType.DMA((2,)),
            ],
        ),
        out_shape=out_shape,
        input_output_aliases=aliases,
        compiler_params=pltpu.CompilerParams(vmem_limit_bytes=VMEM_LIMIT),
        cost_estimate=pl.CostEstimate(
            flops=12 * 5 * times * strip * size * width, bytes_accessed=24 << 20, transcendentals=0
        ),
        name=name,
    )(meta, coef, *args)


def chain_kernel(block, *refs):
    at, spots = refs[:2]
    parts, (v_high, v_low, near_ref, far_ref) = refs[2:-14], refs[-14:-10]
    pf, wh, wl, lh, ll, xf, sem_p, sem_v, sem_r, sem_o = refs[-10:]
    n = pf.shape[0]
    m = lh.shape[1]
    blocks = n // block
    size = parts[0].shape[2]
    row = pl.multiple_of(at[0], 16)
    row_copies = [
        pltpu.make_async_copy(v_high.at[pl.ds(row, m), :], lh.at[0], sem_r.at[0]),
        pltpu.make_async_copy(v_low.at[pl.ds(row, m), :], ll.at[0], sem_r.at[1]),
    ]
    p_copies = []
    for part in parts:
        for t in range(part.shape[0]):
            k = len(p_copies)
            i = pl.multiple_of(spots[2 * k], 16)
            j = pl.multiple_of(spots[2 * k + 1], 128)
            there = pf.at[pl.ds(i, part.shape[1]), pl.ds(j, size)]
            p_copies.append(pltpu.make_async_copy(part.at[t], there, sem_p))

    def v_copies(b):
        cols = pl.ds(pl.multiple_of(b * block, block), block)
        return [
            pltpu.make_async_copy(v_high.at[:, cols], wh.at[1, :, cols], sem_v.at[0, b]),
            pltpu.make_async_copy(v_low.at[:, cols], wl.at[1, :, cols], sem_v.at[1, b]),
        ]

    for copy in p_copies + row_copies:
        copy.start()
    for copy in p_copies:
        copy.wait()
    for b in range(blocks):
        for copy in v_copies(b):
            copy.start()

    def mirror(j, _):
        def one(i, _):
            rows, cols = (pl.ds(pl.multiple_of(s * size, 128), size) for s in (i, j))
            pf[cols, rows] = pf[rows, cols].T
            return 0

        return lax.fori_loop(0, j, one, 0)

    lax.fori_loop(1, n // size, mirror, 0)

    def split_rows(i, _):
        rows = pl.ds(pl.multiple_of(i * 128, 128), 128)
        wh[0, rows], wl[0, rows] = halves(pf[rows, :])
        return 0

    lax.fori_loop(0, n // 128, split_rows, 0)

    for copy in row_copies:
        copy.wait()

    def body(k, _):
        stage, b = lax.div(k, blocks), lax.rem(k, blocks)
        this = lax.rem(stage, 2)
        cols = pl.ds(pl.multiple_of(b * block, block), block)

        @pl.when(stage == 1)
        def _():
            for copy in v_copies(b):
                copy.wait()

        r = dot3(lh[this], ll[this], wh[this, :, cols], wl[this, :, cols])
        r = r + jnp.where(stage == 2, xf[this, :, cols], 0.0)
        xf[this, :, cols] = r
        lh[1 - this, :, cols], ll[1 - this, :, cols] = halves(r)

        @pl.when(stage == 3)
        def _():
            src = xf.at[1, :, cols]
            for out, mine in ((near_ref, True), (far_ref, False)):

                @pl.when((at[1] == b) == mine)
                def _(out=out):
                    pltpu.make_async_copy(src, out, sem_o.at[b]).start()

        return 0

    lax.fori_loop(0, 4 * blocks, body, 0)
    for h in range(blocks):
        pltpu.make_async_copy(xf.at[1, :, : block], near_ref, sem_o.at[h]).wait()


def chain(at, spots, parts, v_high, v_low, rows, cols):
    n = v_high.shape[0]
    blocks = n // cols
    smem, hbm = pl.BlockSpec(memory_space=pltpu.SMEM), pl.BlockSpec(memory_space=pl.ANY)
    scratch = [pltpu.VMEM((n, n), F32)] + [pltpu.VMEM((2, n, n), BF16)] * 2
    scratch += [pltpu.VMEM((2, rows, n), BF16)] * 2 + [pltpu.VMEM((2, rows, n), F32)]
    scratch += [pltpu.SemaphoreType.DMA, pltpu.SemaphoreType.DMA((2, blocks))]
    scratch += [pltpu.SemaphoreType.DMA((2,)), pltpu.SemaphoreType.DMA((blocks,))]
    return pl.pallas_call(
        functools.partial(chain_kernel, cols),
        in_specs=[smem] * 2 + [hbm] * (len(parts) + 2),
        out_specs=[hbm] * 2,
        out_shape=[jax.ShapeDtypeStruct((rows, cols), F32)] * 2,
        scratch_shapes=scratch,
        compiler_params=pltpu.CompilerParams(vmem_limit_bytes=VMEM_LIMIT),
        cost_estimate=pl.CostEstimate(flops=24 * rows * n * n, bytes_accessed=20 << 20, transcendentals=0),
        name="chain",
    )(at, spots, *parts, v_high, v_low)


def move(v, where):
    cols = lax.axis_size("col")
    pairs = []
    for r in range(lax.axis_size("row")):
        for c in range(cols):
            x, y, core = where(c, r // 2, r % 2)
            pairs.append((r * cols + c, (2 * y + core) * cols + x))
    return lax.ppermute(v, ("row", "col"), pairs)


def over(v, dx, dy, dc):
    return move(v, lambda x, y, c: (x ^ dx, y ^ dy, c ^ dc))


def ring(v, steps=1):
    size = lax.axis_size("tm")
    return lax.ppermute(v, "tm", [(i, (i + steps) % size) for i in range(size)])


def together(*values):
    return lax.optimization_barrier(values)


def after(v, *others):
    return together(v, *others)[0]


def tables_of(size, tile_rows):
    strip = size // 4
    devices = [(x, y, c) for y in range(2) for c in range(2) for x in range(2)]

    def strips(x, y, c):
        return [2 * c, 2 * c + 1, 2 * x + c, 2 * y + c, 2 * x + c]

    def spots(x, y, c):
        cross = y ^ (1 - x)
        left = [2 * x + y, y, 2 * x, cross]
        right = [2 * x + y, 2 + y, 2 * x + 1, 3 - cross]
        return [(a * size + t * strip, b * size) for a, b, t in zip(left, right, strips(x, y, c)[:1] + strips(x, y, c)[2:])]

    meta, places, at = [], [], []
    for x, y, c in devices:
        sets = [2 * x + y, 2 * (1 - x) + y, 2 * x + 1 - y]
        left, right = [0, 0, x, 2 * y, 2 - x], [0, 0, 1 - x, 2 - 2 * y, 1 + x]
        meta.append(
            [c * 2 * strip, (1 - c) * 2 * strip]
            + [s * size for s in sets]
            + [s * size + t * strip for s, t in zip(left, strips(x, y, c))]
            + [s * size for s in right]
        )
        at.append([[(2 * c + (y ^ e)) * tile_rows, x] for e in range(2)])
        places.append(
            [spots(x ^ dx, y ^ dy, c ^ dc) for dc in range(2) for dx in range(2) for dy in range(2)]
        )
    flat = np.array(places, np.int32).reshape(len(devices), -1)
    return np.array(meta, np.int32), flat, np.array(at, np.int32)


def on_plane(c_occ, c_vir, eps_occ, eps_vir, tau, tweight, omega, coulomb):
    grid = coulomb.shape[0]
    planes = lax.axis_size("tm")
    rows_n, cols_n = lax.axis_size("row"), lax.axis_size("col")
    z, r, x = lax.axis_index("tm"), lax.axis_index("row"), lax.axis_index("col")
    y, core = r // 2, r % 2
    tile_rows, tile_cols = grid // rows_n, grid // cols_n
    size = grid // 4
    strip = size // 4
    ways = [(dx, dy) for dx in range(2) for dy in range(2)]
    here = (2 * y + core) * cols_n + x
    meta_of, spots_of, at_of = tables_of(size, tile_rows)
    meta = jnp.array(meta_of)[here]

    energies = jnp.stack([eps_occ, -eps_vir])
    arriving = [ring(energies, t) for t in range(1, planes)]

    def factor(e):
        return jnp.exp(e[None, :] * tau[:, None])

    gamma = tweight[None, :] * jnp.cos(omega[:, None] * tau[None, :])
    per_plane = omega.shape[0] // planes
    coef = -2.0 * jnp.stack(
        [gamma[z * per_plane + 2 * (x ^ dx) + (y ^ dy)] for dx, dy in ways]
    )

    start = (2 * x + y) * size + core * 2 * strip
    common = (meta, coef, size)
    piece = jnp.stack([lax.dynamic_slice_in_dim(c, start, 2 * strip, 0) for c in (c_occ, c_vir)])
    part = c_occ.shape[1]
    v_high, v_low = split(coulomb)

    def to_neighbours(v):
        return [over(v, 1, 0, 0), over(v, 0, 1, 0)]

    def with_other_core(near):
        return near + [over(v, 0, 0, 1) for v in near]

    arrived, v_high, v_low, *arriving = together(ring(piece), v_high, v_low, *arriving)
    factors = jnp.stack([factor(e) for e in jnp.concatenate(arriving, axis=1)])
    own = [after(c_occ, arrived), c_vir]
    green = green_call("green_own", own, jnp.stack([factor(e) for e in energies]), *common)
    near, sets = [arrived], []
    for t in range(2, planes):
        *near, arrived, green = together(*near, *to_neighbours(near[0]), ring(near[0]), green)
        sets.append(with_other_core(near))
        near = [arrived]
        if t == 3:
            sets[0] = list(together(*sets[0], arrived))[:-1]
    *near, green = together(
        *near,
        *to_neighbours(near[0]),
        green_call("green_first", sets[0], factors[:, :, :part], *common, green),
    )
    rest = sum(sets[1:], []) + with_other_core(near)
    rest = functools.partial(green_call, "green_rest", rest, factors[:, :, part:], *common)

    def to_chips(parts):
        return [over(p, dx, dy, 0) if dx + dy else p for p, (dx, dy) in zip(parts, ways)]

    some = rest(green, True, range(SOME))
    more = rest(after(green, *some), True, range(SOME, 5))
    both = together(*to_chips(some), *more)
    some, more = both[: len(ways)], both[len(ways) :]
    here, _ = together(here, more[0])
    spots, at = jnp.array(spots_of)[here], jnp.array(at_of)[here]
    more, spots, at = together(to_chips(more), spots, at)
    some = [p.reshape(1, SOME * strip, size) for p in some]
    parts = [p for pair in zip(some, more) for p in pair]
    parts += [over(p, 0, 0, 1) for p in parts]

    arrivals = []
    for e in range(2):
        near, far = chain(at[e], spots, parts, v_high, v_low, tile_rows, tile_cols)
        for dx, value in ((1 - e, (near, far)[1 - e]), (e, (near, far)[e])):
            value = move(value, lambda x, y, c, dx=dx, e=e: (x ^ dx, c, y ^ e))
            arrivals.append((2 * (x ^ dx) + (core ^ e), value))
    out = jnp.zeros((per_plane, tile_rows, tile_cols), F32)
    for k, value in arrivals:
        out = lax.dynamic_update_slice(out, value[None], (k, 0, 0))
    return out


def green_block(rows_c, cols_c, energies, taus, sign):
    factor = jnp.exp(sign * taus[:, None] * energies[None, :])
    width = rows_c.shape[1]
    scaled = rows_c[:, None, :] * factor[None, :, :]
    lead = (rows_c.shape[0], taus.shape[0])
    flat = scaled.reshape(lead[0] * lead[1], width)
    product = lax.dot_general(
        flat, cols_c, (((1,), (1,)), ((), ())), precision=HIGH, preferred_element_type=F32
    )
    return product.reshape(lead[0], lead[1], cols_c.shape[0])


def on_device(c_occ, c_vir, eps_occ, eps_vir, tau, tweight, omega, coulomb):
    grid = coulomb.shape[0]
    tile_rows = grid // lax.axis_size("row")
    tile_cols = grid // lax.axis_size("col")
    row_start = lax.axis_index("row") * tile_rows
    col_start = lax.axis_index("col") * tile_cols
    occ_rows = lax.dynamic_slice_in_dim(c_occ, row_start, tile_rows, 0)
    occ_cols = lax.dynamic_slice_in_dim(c_occ, col_start, tile_cols, 0)
    vir_rows = lax.dynamic_slice_in_dim(c_vir, row_start, tile_rows, 0)
    vir_cols = lax.dynamic_slice_in_dim(c_vir, col_start, tile_cols, 0)
    gamma = tweight[None, :] * jnp.cos(omega[:, None] * tau[None, :])
    green_occ = green_block(occ_rows, occ_cols, eps_occ, tau, 1.0)
    green_vir = green_block(vir_rows, vir_cols, eps_vir, tau, -1.0)
    greens = lax.psum_scatter(
        jnp.stack([green_occ, green_vir], axis=1), "tm", scatter_dimension=0, tiled=True
    )
    polar_time = -2.0 * greens[:, 0] * greens[:, 1]
    polar_all = jnp.einsum("kj,ijc->kic", gamma, polar_time, precision=HIGH)
    polar = lax.all_to_all(polar_all, "tm", split_axis=0, concat_axis=1, tiled=True)
    coulomb_rows = lax.dynamic_slice_in_dim(coulomb, row_start, tile_rows, 0)
    coulomb_cols = lax.dynamic_slice_in_dim(coulomb, col_start, tile_cols, 1)
    coulomb_tile = lax.dynamic_slice_in_dim(coulomb_rows, col_start, tile_cols, 1)
    coupled = jnp.einsum(
        "ik,fkj->fij", coulomb_rows, lax.all_gather(polar, "row", axis=1, tiled=True), precision=HIGH
    )
    coupled_rows = lax.all_gather(coupled, "col", axis=2, tiled=True)
    first = coulomb_tile[None] + jnp.einsum(
        "fik,kj->fij", coupled_rows, coulomb_cols, precision=HIGH
    )
    return jnp.einsum(
        "fik,fkj->fij", coupled_rows, lax.all_gather(first, "row", axis=1, tiled=True), precision=HIGH
    )


def solution(mesh):
    in_specs = (P(None, "tm"), P(None, "tm"), P("tm"), P("tm"), P(), P(), P(), P())
    out_specs = P("tm", "row", "col")
    square = mesh.shape["row"] == 4 and mesh.shape["col"] == 2

    def body(*args):
        omega, coulomb = args[6], args[7]
        fits = omega.shape[0] == 2 * mesh.shape["tm"] * mesh.shape["col"]
        fits = fits and coulomb.shape[0] % (6 * TILE) == 0 and args[0].shape[1] % 128 == 0
        return (on_plane if square and fits else on_device)(*args)

    return jax.shard_map(
        body, mesh=mesh, in_specs=in_specs, out_specs=out_specs, check_vma=False
    )
```
